256 devices in a mesh: blk: 64 (over x_lo, z, y), rep: 4 (over x_hi, core).
Axes of the slice: x: 4 (x_hi: 2, x_lo: 2; x = x_hi * 2 + x_lo), y: 4, z: 8, core: 2. Of those that a mesh axis runs over, the one named last changes fastest.
Arguments:
- entity: bfloat16 [32768, 512], P('blk'), may hold values from -1.1953125 to 1.1953125
- relation: bfloat16 [16, 512, 512], P('rep'), may hold values from -0.25 to 0.25
- head_owner: int32 [65536, 1], P(('blk', 'rep')), may hold values from 0 to 63; in each aligned block of 256 rows (0 to 255, 256 to 511, ...) at most 8 rows name the same one
- head_row: int32 [65536], P(('blk', 'rep')), may hold values from 0 to 511
- query_rel: int32 [65536, 4], P(('blk', 'rep')), may hold values from 0 to 3
- tail_row: int32 [65536, 4], P(('blk', 'rep')), may hold values from 0 to 511
- neg_row: int32 [64, 1024], P('blk', 'rep'), may hold values from 0 to 511
Outputs:
- grad_entity: float32 [32768, 512], P('blk', 'rep')
- grad_rel: float32 [16, 512, 512], P('rep', 'blk')
The draws below stay inside these ranges and needn't reach their ends.
Inputs may be any that keep to these rules, and one draw needn't show every extreme that they name: `head_owner`: in each aligned block of 256 rows (the heads of one group) no shard number appears more than 8 times.
All inputs are finite; a program needn't handle non-finite values.
Results may differ from the reference program's by a relative error of at most 0.0035.
Values may be sent and summed in bfloat16 or wider, within the bound.
A program may use at most 64 MiB of HBM per device.

```python
import math
import jax
import jax.numpy as jnp
import numpy as np
from jax import lax

D = 512
ENT_DEV = 512
HEAD_DEV = 256
QPH = 4
REL_DEV = 4
NEG_ROWS = 256
STOPS = 6
SHARDS = 64
GROUPS = 4
NENT = 32768
REL = 16
HEADS = 65536
CAP = 8
FWD = 3
BACK = 2


def touch_ends(values, own_key, low, high):
    index_at = [jax.random.randint(jax.random.fold_in(own_key, axis), (), 0, length) for axis, length in enumerate(values.shape)]
    widest = values.shape.index(max(values.shape))
    beside = index_at[:widest] + [(index_at[widest] + 1) % values.shape[widest]] + index_at[widest + 1:]
    return values.at[tuple(index_at)].set(low).at[tuple(beside)].set(high)


def level_of(rng, shape, cuts, least, largest):
    def one(axis_at, parts):
        heights = jax.random.uniform(jax.random.fold_in(jax.random.fold_in(rng, 6), axis_at), (parts,), jnp.float32, least / len(cuts), largest / len(cuts))
        return jnp.repeat(jnp.exp(heights), shape[axis_at] // parts).reshape((-1,) + (1,) * (len(shape) - axis_at - 1))

    level = one(*cuts[0])
    for cut in cuts[1:]:
        level = level * one(*cut)
    return level


def deal_out(stream_key, own, number, rows, count, top, bound, slope):
    sequence = jax.random.permutation(stream_key, count)
    packed, ordinary = shares(count, rows * top, bound, slope, True), shares(count, rows * top, bound, slope, False)
    places = jnp.arange(count)

    def named(lengths, offset_by):
        used = int((lengths > 0).sum())
        fixed = max(1, used // 4)
        moved = fixed + (places - fixed + offset_by * (used - fixed)) % max(1, count - fixed)
        return jnp.zeros((count,), jnp.int32).at[sequence[jnp.where(places < fixed, places, moved)]].set(jnp.asarray(lengths, jnp.int32))

    lengths = jnp.where(number % 4 == 0, named(packed, number // 4), named(ordinary, number - number // 4 - 1))
    mixed = jax.random.permutation(jax.random.fold_in(own, 3), count)
    giver, sink = mixed[0:count // 2 * 2:2], mixed[1:count // 2 * 2:2]
    room = jnp.minimum(lengths[giver] - 1, bound - lengths[sink]) // 2
    room = jnp.where((giver == sequence[0]) | (sink == sequence[0]) | (lengths[sink] == 0), 0, jnp.maximum(room, 0))
    moved = jax.random.randint(jax.random.fold_in(own, 4), (count // 2,), 0, 1 << 20) % (room + 1)
    lengths = lengths.at[giver].add(-moved).at[sink].add(moved)
    items = jnp.searchsorted(jnp.cumsum(lengths), jnp.arange(rows * top), side="right").astype(jnp.int32)
    table = items.reshape(top, rows).T
    table = table[jax.random.permutation(jax.random.fold_in(own, 1), rows)]
    offset_by = jax.random.randint(jax.random.fold_in(own, 2), (rows, 1), 0, top)
    return jnp.take_along_axis(table, (jnp.arange(top)[None, :] + offset_by) % top, axis=1)


def shares(number_of, total, bound, slope, full):
    portions = [(1 << 20) // math.isqrt(rank ** slope) + 1 for rank in range(1, number_of + 1)]
    largest = bound if full else min(bound, max(-(-total // number_of), total * portions[0] // sum(portions)))
    least = 1 if total - largest >= number_of - 1 else 0
    given, rest = [largest] + [least] * (number_of - 1), total - largest - least * (number_of - 1)
    while rest > 0:
        candidates = [i for i in range(1, number_of) if given[i] < largest] or [i for i in range(1, number_of) if given[i] < bound]
        mass, remaining = sum([portions[i] for i in candidates]), rest
        for i in candidates:
            extra = min(bound - given[i], max(1, remaining * portions[i] // mass), rest)
            given[i] = given[i] + extra
            rest = rest - extra
    return np.array(given)


def noise(key, shape, spread, limit, cuts=(), held_as=jnp.bfloat16):
    result = jax.random.normal(key, shape, jnp.float32) * spread
    if len(cuts) > 0:
        result = level_of(key, shape, cuts, -0.22, 0.18) * result
    return jnp.clip(result, min=-limit, max=limit).astype(held_as)


def setup_inputs(seed: int = 0) -> dict:
    keys = jax.random.split(jax.random.key(seed), 8)
    entity = noise(keys[0], (NENT, D), 0.2, 1.1953125, ((0, 64),))
    relation = noise(keys[1], (REL, D, D), D ** -0.5, 0.25, ((0, 4),))
    head_owner_keys = jax.random.split(jax.random.fold_in(keys[2], 1), HEADS // HEAD_DEV)
    head_owner_turns = jax.random.permutation(jax.random.fold_in(keys[2], 3), HEADS // HEAD_DEV)
    head_owner = jax.vmap(lambda own, number: deal_out(jax.random.fold_in(keys[2], 2), own, number, HEAD_DEV, SHARDS, 1, CAP, 2))(head_owner_keys, head_owner_turns).reshape((HEADS, 1))
    head_row = touch_ends(jax.random.randint(keys[3], (HEADS,), 0, ENT_DEV), jax.random.fold_in(keys[3], 1), 0, ENT_DEV - 1).astype(jnp.int32)
    query_rel = touch_ends(jax.random.randint(keys[4], (HEADS, QPH), 0, REL_DEV), jax.random.fold_in(keys[4], 1), 0, REL_DEV - 1).astype(jnp.int32)
    tail_row = touch_ends(jax.random.randint(keys[5], (HEADS, QPH), 0, ENT_DEV), jax.random.fold_in(keys[5], 1), 0, ENT_DEV - 1).astype(jnp.int32)
    neg_row = touch_ends(jax.random.randint(keys[6], (SHARDS, GROUPS * NEG_ROWS), 0, ENT_DEV), jax.random.fold_in(keys[6], 1), 0, ENT_DEV - 1).astype(jnp.int32)
    return dict(entity=entity, relation=relation, head_owner=head_owner, head_row=head_row, query_rel=query_rel, tail_row=tail_row, neg_row=neg_row)


def reference(entity, relation, head_owner, head_row, query_rel, tail_row, neg_row):
    group_total = SHARDS * GROUPS
    heads_all = (head_owner[:, 0] * ENT_DEV + head_row).astype(jnp.int32).reshape(group_total, HEAD_DEV)
    rel_all = query_rel.reshape(group_total, HEAD_DEV, QPH)
    tail_all = tail_row.reshape(group_total, HEAD_DEV, QPH)
    shard_base = (jnp.arange(SHARDS, dtype=jnp.int32) * ENT_DEV)[:, None, None]
    neg_ids = (neg_row.reshape(SHARDS, GROUPS, NEG_ROWS) + shard_base).astype(jnp.int32)

    def group_step(state_pair, inputs):
        grad_table, grad_rel = state_pair
        group_index, head_ids, rel_ids, tail_local = inputs
        shard_index = group_index // GROUPS
        rel_group = group_index % GROUPS
        head_vec = jnp.take(entity, head_ids, axis=0)
        rel_mats = lax.dynamic_slice_in_dim(relation, (rel_group * REL_DEV).astype(jnp.int32), REL_DEV, 0)
        queries = jnp.zeros((HEAD_DEV, QPH, D), jnp.float32)
        for rel_index in range(REL_DEV):
            product = jnp.dot(head_vec, rel_mats[rel_index], preferred_element_type=jnp.float32)
            queries = queries + jnp.where((rel_ids == rel_index)[:, :, None], product[:, None, :], 0.0)
        queries = queries.astype(jnp.bfloat16).reshape(HEAD_DEV * QPH, D)
        tail_ids = (shard_index * ENT_DEV + tail_local).reshape(-1).astype(jnp.int32)
        tail_vec = jnp.take(entity, tail_ids, axis=0)
        pos_score = jnp.sum(queries.astype(jnp.float32) * tail_vec.astype(jnp.float32), axis=1)
        pos_weight = jax.nn.sigmoid(pos_score) - 1.0
        grad_query = pos_weight[:, None] * tail_vec.astype(jnp.float32)
        grad_table = grad_table.at[tail_ids].add(pos_weight[:, None] * queries.astype(jnp.float32))
        for offset in range(-BACK, FWD + 1):
            owner_shard = (shard_index - offset) % SHARDS
            block_ids = neg_ids[owner_shard, rel_group]
            neg_block = jnp.take(entity, block_ids, axis=0)
            neg_score = jnp.dot(queries, neg_block.T, preferred_element_type=jnp.float32)
            neg_weight = (jax.nn.sigmoid(neg_score) / STOPS).astype(jnp.bfloat16)
            grad_query = grad_query + jnp.dot(neg_weight, neg_block, preferred_element_type=jnp.float32)
            grad_table = grad_table.at[block_ids].add(jnp.dot(neg_weight.T, queries, preferred_element_type=jnp.float32))
        grad_query = grad_query.reshape(HEAD_DEV, QPH, D)
        grad_head = jnp.zeros((HEAD_DEV, D), jnp.float32)
        for rel_index in range(REL_DEV):
            grad_pair = jnp.sum(jnp.where((rel_ids == rel_index)[:, :, None], grad_query, 0.0), axis=1).astype(jnp.bfloat16)
            grad_head = grad_head + jnp.dot(grad_pair, rel_mats[rel_index].T, preferred_element_type=jnp.float32)
            grad_rel = grad_rel.at[rel_group * REL_DEV + rel_index].add(jnp.dot(head_vec.T, grad_pair, preferred_element_type=jnp.float32))
        grad_table = grad_table.at[head_ids].add(grad_head)
        return (grad_table, grad_rel), None

    start = (jnp.zeros((NENT, D), jnp.float32), jnp.zeros((REL, D, D), jnp.float32))
    groups_iota = jnp.arange(group_total, dtype=jnp.int32)
    final, unused = lax.scan(group_step, start, (groups_iota, heads_all, rel_all, tail_all))
    return final[0], final[1]
```

```python
import functools

import jax
import jax.numpy as jnp
from jax import lax
from jax.experimental import pallas as pl
from jax.experimental.pallas import tpu as pltpu
from jax.sharding import PartitionSpec as P

D = 512
STOPS = 6
NBLK, NY, NZ, NX, NREP = 64, 4, 8, 2, 4
OFFS = (0, 1, -1, 3, 2, -2)
MESH = pl.DeviceIdType.MESH
F32, BF16, I32 = jnp.float32, jnp.bfloat16, jnp.int32
NT = (((1,), (1,)), ((), ()))
TN = (((0,), (0,)), ((), ()))


def iota(shape, dim):
    return lax.broadcasted_iota(I32, shape, dim)


def hot(mask):
    return jnp.where(mask, 1.0, 0.0).astype(BF16)


def mm(a, b):
    return jnp.dot(a, b, preferred_element_type=F32)


def mm_nt(a, b):
    return lax.dot_general(a, b, NT, preferred_element_type=F32)


def mm_tn(a, b):
    return lax.dot_general(a, b, TN, preferred_element_type=F32)


def two_parts(value):
    high = value.astype(BF16)
    return high, (value - high.astype(F32)).astype(BF16)


def kernel(
    ent, rel, cols, rows, out_e, out_r,
    asked, wanted, wanted2, w_row, served, fetched, blocks, tails, head, head_t, head_p,
    prod, query, pos_w, grad_q, pair, pair_p, term, term_own, term_s, term_r, back_s, back_r,
    rel_f, rel_s, rel_y, rz_f, rz_s, rz_r, rx_s, rx_r, loc, loc_s, loc_r,
    a2a_sem, nb_sem, gt_sem, x_sem, y_sem, z_sem, rep_sem,
):
    b, r = lax.axis_index("blk"), lax.axis_index("rep")
    y, z, xl = lax.rem(b, NY), lax.rem(lax.div(b, NY), NZ), lax.div(b, NY * NZ)
    xp = 1 - xl
    other_x = lax.rem(b + NY * NZ, NBLK)

    def send(src, dst, s_sem, r_sem, blk, rep):
        copy = pltpu.make_async_remote_copy(
            src_ref=src, dst_ref=dst, send_sem=s_sem, recv_sem=r_sem, device_id=(blk, rep), device_id_type=MESH
        )
        copy.start()
        return copy

    def wait_all(ref, sem):
        pltpu.make_async_copy(ref, ref, sem).wait()

    def to_all(src, dst, s_sem, r_sem):
        def step(k, carry):
            peer = lax.rem(b + k, NBLK)
            send(src(peer), dst, s_sem, r_sem, peer, r)
            return carry

        lax.fori_loop(1, NBLK, step, 0)

    def rows16(ref):
        return lambda s: ref.at[pl.ds(pl.multiple_of(s * 16, 16), 16)]

    barrier = pltpu.get_barrier_semaphore()

    def greet(k, carry):
        pl.semaphore_signal(barrier, inc=1, device_id=(lax.rem(b + k, NBLK), r), device_id_type=MESH)
        return carry

    lax.fori_loop(1, NBLK, greet, 0)
    for d in range(1, NREP):
        pl.semaphore_signal(barrier, inc=1, device_id=(b, lax.rem(r + d, NREP)), device_id_type=MESH)

    owner_row, owner_col = rows[0:1, :], cols[:, 0:1]
    in_shard = iota((NBLK, 256), 0) == owner_row
    shard_hot = hot(in_shard)
    before = mm(shard_hot, hot(iota((256, 256), 0) < iota((256, 256), 1)))
    slot_row = jnp.sum(jnp.where(in_shard, before, 0.0), axis=0, keepdims=True)
    place_row = owner_row * 16 + slot_row.astype(I32)
    of_head = iota((256, 128), 1) == owner_col
    before = mm(hot(iota((256, 256), 1) < iota((256, 256), 0)), hot(of_head))
    slot_col = jnp.sum(jnp.where(of_head, before, 0.0), axis=1, keepdims=True).astype(I32)
    place_col = owner_col * 16 + slot_col
    named = cols[:, 1:2] + 1
    lane = iota((256, 128), 1)
    digits = jnp.where(lane == slot_col, named >> 5, 0) + jnp.where(lane == slot_col + 64, named & 31, 0)
    requests = mm(shard_hot, digits.astype(F32).astype(BF16))
    for s in range(NBLK):
        asked[s] = requests[s : s + 1, :]
    blocks[0] = mm(hot(iota((256, D), 1) == cols[:, 10:11]), ent[...]).astype(BF16)

    pl.semaphore_wait(barrier, NBLK - 1 + NREP - 1)
    to_all(lambda s: asked.at[s], wanted.at[b], a2a_sem.at[0], a2a_sem.at[1])
    wanted[b] = asked[b]
    for j in range(2):
        tails[j] = mm(hot(iota((256, D), 1) == cols[:, 6 + j : 7 + j]), ent[...]).astype(BF16)
    wait_all(wanted.at[pl.ds(0, NBLK - 1)], a2a_sem.at[1])

    for s in range(NBLK):
        wanted2[s : s + 1, :] = wanted[s]
    spread = mm(hot(iota((1024, NBLK), 0) >> 4 == iota((1024, NBLK), 1)), wanted2[...].astype(BF16))
    k_of, lane = iota((1024, 128), 0) & 7, iota((1024, 128), 1)
    spread = jnp.where(lane == k_of, spread * 32.0, jnp.where(lane == k_of + 64, spread, 0.0))
    w_row[...] = mm_nt(jnp.ones((8, 128), BF16), spread.astype(BF16)).astype(I32) - 1
    w_col = jnp.sum(spread, axis=1, keepdims=True).astype(I32) - 1
    first_half = (iota((256, 256), 0) >> 3 & 1) == 0
    for t in range(4):
        whole = mm(hot(iota((256, D), 1) == w_col[t * 256 : (t + 1) * 256]), ent[...])
        served[t * 256 : (t + 1) * 256] = jnp.where(first_half, whole[:, :256], whole[:, 256:]).astype(BF16)
    mine = pl.ds(pl.multiple_of(b * 16, 16), 16)
    to_all(rows16(served), fetched.at[mine], a2a_sem.at[2], a2a_sem.at[3])
    block_out = []
    for n in range(1, STOPS):
        visitor = lax.rem(b + OFFS[n] + NBLK, NBLK)
        block_out.append(send(blocks.at[0], blocks.at[n], nb_sem.at[n - 1], nb_sem.at[4 + n], visitor, r))
    fetched[mine] = served[mine]
    for j in range(2, 4):
        tails[j] = mm(hot(iota((256, D), 1) == cols[:, 6 + j : 7 + j]), ent[...]).astype(BF16)
    wait_all(fetched.at[pl.ds(0, (NBLK - 1) * 16)], a2a_sem.at[3])
    for h in range(2):
        picked = hot(iota((256, 1024), 1) == place_col + 8 * h)
        head[:, h * 256 : (h + 1) * 256] = mm(picked, fetched[...]).astype(BF16)

    for k in range(4):
        prod[k] = mm(head[...], rel[k])

    def query_rows(t, carry):
        at = pl.ds(pl.multiple_of(t * 16, 16), 16)
        kind = cols[at, :]
        for j in range(4):
            q = prod[0, at, :]
            for k in range(1, 4):
                q = jnp.where(kind[:, 2 + j : 3 + j] == k, prod[k, at, :], q)
            q = q.astype(BF16)
            query[j, at, :] = q
            tail = tails[j, at, :].astype(F32)
            score = jnp.sum(q.astype(F32) * tail, axis=1, keepdims=True)
            weight = jax.nn.sigmoid(score) - 1.0
            grad_q[j, at, :] = weight * tail
            pos_w[j, at, :] = jnp.broadcast_to(weight, (16, 128))
        return carry

    lax.fori_loop(0, 16, query_rows, 0)

    c = iota((D, D), 0)
    natural = (c >> 3 & 1) * 256 + (c >> 4 & 7) * 32 + (c >> 7) * 8 + (c & 7)
    head_t[...] = mm_nt(hot(iota((D, D), 1) == natural), head[...]).astype(BF16)
    head_out = send(head_t, head_p, x_sem.at[0], x_sem.at[1], other_x, r)

    term_out = []
    for n in range(STOPS):
        if n:
            block_out[n - 1].wait_recv()
        acc = term if n else term_own
        acc[...] = jnp.zeros_like(acc)

        def visit(j, carry, n=n, acc=acc):
            q, block = query[j], blocks[n]
            weight = (jax.nn.sigmoid(mm_nt(q, block)) / STOPS).astype(BF16)
            grad_q[j] += mm(weight, block)
            acc[...] += mm_tn(weight, q)
            return carry

        lax.fori_loop(0, 4, visit, 0)
        if n:
            term_s[n - 1] = term[...].astype(BF16)
            owner = lax.rem(b - OFFS[n] + NBLK, NBLK)
            term_out.append(send(term_s.at[n - 1], term_r.at[n - 1], gt_sem.at[n - 1], gt_sem.at[4 + n], owner, r))

    def pair_rows(t, carry):
        at = pl.ds(pl.multiple_of(t * 16, 16), 16)
        kind = cols[at, :]
        for k in range(4):
            total = jnp.zeros((16, D), F32)
            for j in range(4):
                total += jnp.where(kind[:, 2 + j : 3 + j] == k, grad_q[j, at, :], 0.0)
            pair[k, at, :] = total.astype(BF16)
        return carry

    lax.fori_loop(0, 16, pair_rows, 0)
    pair_out = send(pair.at[pl.ds(2 * xp, 2)], pair_p, x_sem.at[2], x_sem.at[3], other_x, r)

    grad_head = mm_nt(pair[0], rel[0])
    for k in range(1, 4):
        grad_head += mm_nt(pair[k], rel[k])
    grad_head = grad_head.astype(BF16)
    for t in range(4):
        q = iota((256, 256), 0) + t * 256
        whole = mm(hot(q - (q >> 3 & 1) * 8 == place_row), grad_head)
        back_s[t * 256 : (t + 1) * 256] = jnp.where(first_half, whole[:, :256], whole[:, 256:]).astype(BF16)
    to_all(rows16(back_s), back_r.at[mine], a2a_sem.at[4], a2a_sem.at[5])
    back_r[mine] = back_s[mine]

    head_out.wait_recv()
    pair_out.wait_recv()
    for k in range(2):
        rel_f[k] = mm(head_t[...], pair[2 * xl + k]) + mm(head_p[...], pair_p[k])
        rel_s[k] = rel_f[k].astype(BF16)
    y_out = []
    for d in range(1, NY):
        yp = lax.rem(y + d, NY)
        part = rel_s.at[:, pl.ds(pl.multiple_of(yp * 128, 128), 128), :]
        y_out.append(send(part, rel_y.at[d - 1], y_sem.at[d - 1], y_sem.at[2 + d], b - y + yp, r))

    for j in range(4):
        onto = hot(iota((D, 256), 0) == rows[6 + j : 7 + j, :])
        high, low = two_parts(pos_w[j, :, 0:1] * query[j].astype(F32))
        part = mm(onto, high) + mm(onto, low)
        for c in range(4):
            loc[c] = part[:, c * 128 : (c + 1) * 128] if j == 0 else loc[c] + part[:, c * 128 : (c + 1) * 128]
    wait_all(back_r.at[pl.ds(0, (NBLK - 1) * 16)], a2a_sem.at[5])
    lanes = iota((D, 1024), 1)
    for h in range(2):
        onto = hot((iota((D, 1024), 0) == w_row[0:1, :]) & ((lanes >> 3 & 1) == h))
        part = mm(onto, back_r[...])
        for c in range(2):
            loc[2 * h + c] += part[:, c * 128 : (c + 1) * 128]
    total = term_own[...]
    for n in range(STOPS - 1):
        term_out[n].wait_recv()
        total += term_r[n].astype(F32)
    onto = hot(iota((D, 256), 0) == rows[10:11, :])
    high, low = two_parts(total)
    part = mm(onto, high) + mm(onto, low)
    for c in range(4):
        loc[c] += part[:, c * 128 : (c + 1) * 128]
        loc_s[c] = loc[c].astype(BF16)
    rep_out = []
    for d in range(1, NREP):
        rp = lax.rem(r + d, NREP)
        rep_out.append(send(loc_s.at[rp], loc_r.at[d - 1], rep_sem.at[d - 1], rep_sem.at[2 + d], b, rp))

    rz_f[...] = rel_f[:, pl.ds(pl.multiple_of(y * 128, 128), 128), :]
    for d in range(1, NY):
        y_out[d - 1].wait_recv()
        rz_f[...] += rel_y[d - 1].astype(F32)
    rz_s[...] = rz_f[...].astype(BF16)
    z_out = []
    for d in range(1, NZ):
        zp = lax.rem(z + d, NZ)
        part = rz_s.at[:, pl.ds(pl.multiple_of(zp * 16, 16), 16), :]
        z_out.append(send(part, rz_r.at[d - 1], z_sem.at[d - 1], z_sem.at[6 + d], b + (zp - z) * NY, r))

    total = loc[r]
    for d in range(1, NREP):
        rep_out[d - 1].wait_recv()
        total += loc_r[d - 1].astype(F32)
    out_e[...] = total

    total = rz_f[:, pl.ds(pl.multiple_of(z * 16, 16), 16), :]
    for d in range(1, NZ):
        z_out[d - 1].wait_recv()
        total += rz_r[d - 1].astype(F32)
    for x in range(NX):
        rx_s[x] = total[:, x * 8 : (x + 1) * 8, :]
    x_out = send(rx_s.at[xp], rx_r, x_sem.at[4], x_sem.at[5], other_x, r)
    for k in range(2):
        out_r[2 * xl + k] = rx_s[xl, k]
    x_out.wait_recv()
    for k in range(2):
        out_r[2 * xp + k] = rx_r[k]

    for copy in (*block_out, head_out, *term_out, pair_out, *y_out, *rep_out, *z_out, x_out):
        copy.wait_send()
    wait_all(asked.at[pl.ds(0, NBLK - 1)], a2a_sem.at[0])
    wait_all(served.at[pl.ds(0, (NBLK - 1) * 16)], a2a_sem.at[2])
    wait_all(back_s.at[pl.ds(0, (NBLK - 1) * 16)], a2a_sem.at[4])


def per_device(entity, relation, head_owner, head_row, query_rel, tail_row, neg_row):
    cols = jnp.concatenate([head_owner, head_row[:, None], query_rel, tail_row, neg_row.T], axis=1)
    rows = cols.T
    vmem = pl.BlockSpec(memory_space=pltpu.VMEM)
    dma = pltpu.SemaphoreType.DMA
    scratch = [
        pltpu.VMEM((NBLK, 1, 128), F32),
        pltpu.VMEM((NBLK, 1, 128), F32),
        pltpu.VMEM((NBLK, 128), F32),
        pltpu.VMEM((8, 1024), I32),
        pltpu.VMEM((1024, 256), BF16),
        pltpu.VMEM((1024, 256), BF16),
        pltpu.VMEM((STOPS, 256, D), BF16),
        pltpu.VMEM((4, 256, D), BF16),
        pltpu.VMEM((256, D), BF16),
        pltpu.VMEM((D, 256), BF16),
        pltpu.VMEM((D, 256), BF16),
        pltpu.VMEM((4, 256, D), F32),
        pltpu.VMEM((4, 256, D), BF16),
        pltpu.VMEM((4, 256, 128), F32),
        pltpu.VMEM((4, 256, D), F32),
        pltpu.VMEM((4, 256, D), BF16),
        pltpu.VMEM((2, 256, D), BF16),
        pltpu.VMEM((256, D), F32),
        pltpu.VMEM((256, D), F32),
        pltpu.VMEM((STOPS - 1, 256, D), BF16),
        pltpu.VMEM((STOPS - 1, 256, D), BF16),
        pltpu.VMEM((1024, 256), BF16),
        pltpu.VMEM((1024, 256), BF16),
        pltpu.VMEM((2, D, D), F32),
        pltpu.VMEM((2, D, D), BF16),
        pltpu.VMEM((NY - 1, 2, 128, D), BF16),
        pltpu.VMEM((2, 128, D), F32),
        pltpu.VMEM((2, 128, D), BF16),
        pltpu.VMEM((NZ - 1, 2, 16, D), BF16),
        pltpu.VMEM((NX, 2, 8, D), F32),
        pltpu.VMEM((2, 8, D), F32),
        pltpu.VMEM((4, D, 128), F32),
        pltpu.VMEM((4, D, 128), BF16),
        pltpu.VMEM((NREP - 1, D, 128), BF16),
        dma((6,)),
        dma((10,)),
        dma((10,)),
        dma((6,)),
        dma((6,)),
        dma((14,)),
        dma((6,)),
    ]
    return pl.pallas_call(
        kernel,
        out_shape=(jax.ShapeDtypeStruct((D, 128), F32), jax.ShapeDtypeStruct((4, 8, D), F32)),
        in_specs=[vmem] * 4,
        out_specs=(vmem, vmem),
        scratch_shapes=scratch,
        compiler_params=pltpu.CompilerParams(
            collective_id=0, has_side_effects=True, vmem_limit_bytes=50 * 2**20
        ),
        name="rescal_step",
    )(entity, relation, cols, rows)


def solution(mesh):
    placed = (
        P("blk", None),
        P("rep", None, None),
        P(("blk", "rep"), None),
        P(("blk", "rep")),
        P(("blk", "rep"), None),
        P(("blk", "rep"), None),
        P("blk", "rep"),
    )
    return jax.shard_map(
        per_device,
        mesh=mesh,
        in_specs=placed,
        out_specs=(P("blk", "rep"), P("rep", "blk", None)),
        check_vma=False,
    )
```

```python
import functools

import jax
import jax.numpy as jnp
from jax import lax
from jax.experimental import pallas as pl
from jax.experimental.pallas import tpu as pltpu
from jax.sharding import PartitionSpec as P

D = 512
STOPS = 6
NBLK, NY, NZ, NX, NREP = 64, 4, 8, 2, 4
OFFS = (0, 1, -1, 2, -2, 3)
MESH = pl.DeviceIdType.MESH
F32, BF16, I32 = jnp.float32, jnp.bfloat16, jnp.int32
NT = (((1,), (1,)), ((), ()))
TN = (((0,), (0,)), ((), ()))


def iota(shape, dim):
    return lax.broadcasted_iota(I32, shape, dim)


def hot(mask):
    return jnp.where(mask, 1.0, 0.0).astype(BF16)


def mm(a, b):
    return jnp.dot(a, b, preferred_element_type=F32)


def mm_nt(a, b):
    return lax.dot_general(a, b, NT, preferred_element_type=F32)


def mm_tn(a, b):
    return lax.dot_general(a, b, TN, preferred_element_type=F32)


def two_parts(value):
    high = value.astype(BF16)
    return high, (value - high.astype(F32)).astype(BF16)


def kernel(
    ent_h, rel_h, owner_h, row_h, kind_h, tail_h, neg_h, out_e, out_r,
    ent, rel, owner_v, row_v, kind_v, tail_v, neg_v, rows, cols, asked, wanted, wanted2, w_row, served, fetched, blocks, relay, tails, head, head_t, head_p,
    prod, query, pos_w, grad_q, weights, pair, pair_p, term_own, term_s, term_r, term_f, relay_s, relay_r, back_s, back_r,
    rel_f, rel_s, rel_y, rz_f, rz_s, rz_r, rx_s, rx_r, loc, loc_s, loc_r,
    in_sem, a2a_sem, nb_sem, gt_sem, hop_sem, x_sem, y_sem, z_sem, rep_sem,
):
    b, r = lax.axis_index("blk"), lax.axis_index("rep")
    y, z, xl = lax.rem(b, NY), lax.rem(lax.div(b, NY), NZ), lax.div(b, NY * NZ)
    xp = 1 - xl
    other_x = lax.rem(b + NY * NZ, NBLK)

    def remote(src, dst, s_sem, r_sem, blk, rep):
        return pltpu.make_async_remote_copy(
            src_ref=src, dst_ref=dst, send_sem=s_sem, recv_sem=r_sem, device_id=(blk, rep), device_id_type=MESH
        )

    def send(*copy_args):
        copy = remote(*copy_args)
        copy.start()
        return copy

    def block(n):
        return blocks.at[pl.ds(n * 256, 256)]

    def wait_all(ref, sem):
        pltpu.make_async_copy(ref, ref, sem).wait()

    def to_all(src, dst, s_sem, r_sem):
        def step(k, carry):
            peer = lax.rem(b + k, NBLK)
            send(src(peer), dst, s_sem, r_sem, peer, r)
            return carry

        lax.fori_loop(1, NBLK, step, 0)

    def rows16(ref):
        return lambda s: ref.at[pl.ds(pl.multiple_of(s * 16, 16), 16)]

    barrier = pltpu.get_barrier_semaphore()

    def greet(k, carry):
        pl.semaphore_signal(barrier, inc=1, device_id=(lax.rem(b + k, NBLK), r), device_id_type=MESH)
        return carry

    lax.fori_loop(1, NBLK, greet, 0)
    for d in range(1, NREP):
        pl.semaphore_signal(barrier, inc=1, device_id=(b, lax.rem(r + d, NREP)), device_id_type=MESH)

    index_in = []
    for n, (src, dst) in enumerate(
        ((owner_h, owner_v), (row_h, row_v), (kind_h, kind_v), (tail_h, tail_v), (neg_h, neg_v))
    ):
        index_in.append(pltpu.make_async_copy(src, dst, in_sem.at[n]))
    ent_in = pltpu.make_async_copy(ent_h, ent, in_sem.at[5])
    rel_in = pltpu.make_async_copy(rel_h, rel, in_sem.at[6])
    for copy in (*index_in, ent_in, rel_in):
        copy.start()
    for copy in index_in:
        copy.wait()
    rows[...] = jnp.zeros_like(rows)
    rows[0:1, :] = owner_v[...]
    rows[1:2, :] = row_v[...]
    rows[2:6, :] = kind_v[...]
    rows[6:10, :] = tail_v[...]
    rows[10:11, :] = neg_v[...]
    cols[...] = jnp.transpose(rows[...])

    owner_row, owner_col = rows[0:1, :], cols[:, 0:1]
    in_shard = iota((NBLK, 256), 0) == owner_row
    shard_hot = hot(in_shard)
    before = mm(shard_hot, hot(iota((256, 256), 0) < iota((256, 256), 1)))
    slot_row = jnp.sum(jnp.where(in_shard, before, 0.0), axis=0, keepdims=True)
    place_row = owner_row * 16 + slot_row.astype(I32)
    of_head = iota((256, 128), 1) == owner_col
    before = mm(hot(iota((256, 256), 1) < iota((256, 256), 0)), hot(of_head))
    slot_col = jnp.sum(jnp.where(of_head, before, 0.0), axis=1, keepdims=True).astype(I32)
    place_col = owner_col * 16 + slot_col
    named = cols[:, 1:2] + 1
    lane = iota((256, 128), 1)
    digits = jnp.where(lane == slot_col, named >> 5, 0) + jnp.where(lane == slot_col + 64, named & 31, 0)
    requests = mm(shard_hot, digits.astype(F32).astype(BF16))
    for s in range(NBLK):
        asked[s] = requests[s : s + 1, :]
    ent_in.wait()
    block(0)[...] = mm(hot(iota((256, D), 1) == cols[:, 10:11]), ent[...]).astype(BF16)
    rel_in.wait()

    pl.semaphore_wait(barrier, NBLK - 1 + NREP - 1)
    to_all(lambda s: asked.at[s], wanted.at[b], a2a_sem.at[0], a2a_sem.at[1])
    wanted[b] = asked[b]

    plane_up, plane_down = lax.rem(b + NY, NBLK), lax.rem(b + NBLK - NY, NBLK)
    up_out = remote(block(0), relay.at[0], hop_sem.at[0], hop_sem.at[1], plane_up, r)
    down_out = remote(block(0), relay.at[1], hop_sem.at[2], hop_sem.at[3], plane_down, r)
    pl.when(y >= 1)(up_out.start)
    pl.when(y <= 1)(down_out.start)
    block_out, block_far = [], []
    for n in range(1, STOPS):
        visitor = b - y + lax.rem(y + OFFS[n] + NY, NY)
        sems = nb_sem.at[n - 1], nb_sem.at[4 + n]
        block_out.append(remote(block(0), block(n), *sems, visitor, r))
        block_far.append(remote(relay.at[0 if OFFS[n] > 0 else 1], block(n), *sems, visitor, r))
        pl.when((y + OFFS[n] >= 0) & (y + OFFS[n] < NY))(block_out[n - 1].start)
    for j in range(2):
        tails[j * 256 : (j + 1) * 256] = mm(hot(iota((256, D), 1) == cols[:, 6 + j : 7 + j]), ent[...]).astype(BF16)
    wait_all(wanted.at[pl.ds(0, NBLK - 1)], a2a_sem.at[1])

    for s in range(NBLK):
        wanted2[s : s + 1, :] = wanted[s]
    spread = mm(hot(iota((1024, NBLK), 0) >> 4 == iota((1024, NBLK), 1)), wanted2[...].astype(BF16))
    k_of, lane = iota((1024, 128), 0) & 7, iota((1024, 128), 1)
    spread = jnp.where(lane == k_of, spread * 32.0, jnp.where(lane == k_of + 64, spread, 0.0))
    w_row[...] = mm_nt(jnp.ones((8, 128), BF16), spread.astype(BF16)).astype(I32) - 1
    w_col = jnp.sum(spread, axis=1, keepdims=True).astype(I32) - 1
    first_half = (iota((256, 256), 0) >> 3 & 1) == 0
    for t in range(4):
        whole = mm(hot(iota((256, D), 1) == w_col[t * 256 : (t + 1) * 256]), ent[...])
        served[t * 256 : (t + 1) * 256] = jnp.where(first_half, whole[:, :256], whole[:, 256:]).astype(BF16)
    mine = pl.ds(pl.multiple_of(b * 16, 16), 16)
    to_all(rows16(served), fetched.at[mine], a2a_sem.at[2], a2a_sem.at[3])
    fetched[mine] = served[mine]
    pl.when(y >= 1)(up_out.wait_recv)
    pl.when(y <= 1)(down_out.wait_recv)
    for n in range(1, STOPS):
        pl.when((y + OFFS[n] < 0) | (y + OFFS[n] >= NY))(block_far[n - 1].start)
    for j in range(2, 4):
        tails[j * 256 : (j + 1) * 256] = mm(hot(iota((256, D), 1) == cols[:, 6 + j : 7 + j]), ent[...]).astype(BF16)
    wait_all(fetched.at[pl.ds(0, (NBLK - 1) * 16)], a2a_sem.at[3])
    for h in range(2):
        picked = hot(iota((256, 1024), 1) == place_col + 8 * h)
        head[:, h * 256 : (h + 1) * 256] = mm(picked, fetched[...]).astype(BF16)

    for k in range(4):
        prod[k] = mm(head[...], rel[k])

    def query_rows(t, carry):
        at = pl.ds(pl.multiple_of(t * 16, 16), 16)
        kind = cols[at, :]
        for j in range(4):
            to = pl.ds(pl.multiple_of(j * 256 + t * 16, 16), 16)
            q = prod[0, at, :]
            for k in range(1, 4):
                q = jnp.where(kind[:, 2 + j : 3 + j] == k, prod[k, at, :], q)
            q = q.astype(BF16)
            query[to, :] = q
            tail = tails[to, :].astype(F32)
            score = jnp.sum(q.astype(F32) * tail, axis=1, keepdims=True)
            weight = jax.nn.sigmoid(score) - 1.0
            grad_q[to, :] = weight * tail
            pos_w[to, :] = jnp.broadcast_to(weight, (16, 128))
        return carry

    lax.fori_loop(0, 16, query_rows, 0, unroll=2)

    c = iota((D, D), 0)
    natural = (c >> 3 & 1) * 256 + (c >> 4 & 7) * 32 + (c >> 7) * 8 + (c & 7)
    head_t[...] = mm_nt(hot(iota((D, D), 1) == natural), head[...]).astype(BF16)
    head_out = send(head_t, head_p, x_sem.at[0], x_sem.at[1], other_x, r)

    term_out = []
    for n in range(STOPS):
        if n:
            block_out[n - 1].wait_recv()
        met = slice(n * 256, (n + 1) * 256)
        weights[:, met] = (jax.nn.sigmoid(mm_nt(query[...], block(n)[...])) * (1.0 / STOPS)).astype(BF16)
        term = mm_tn(weights[:, met], query[...])
        if n == 0:
            term_own[...] = term
        else:
            term_s[n - 1] = term.astype(BF16)
            via = b - y + lax.rem(y - OFFS[n] + NY, NY)
            term_out.append(send(term_s.at[n - 1], term_r.at[n - 1], gt_sem.at[n - 1], gt_sem.at[4 + n], via, r))
        for upto, since in ((4, 0), (STOPS, 4)):
            if n == upto - 1:
                met = slice(since * 256, upto * 256)
                for j in range(4):
                    at = slice(j * 256, (j + 1) * 256)
                    grad_q[at, :] += mm(weights[at, met], blocks[met, :])

    def pair_rows(t, carry):
        at = pl.ds(pl.multiple_of(t * 16, 16), 16)
        kind = cols[at, :]
        for k in range(4):
            total = jnp.zeros((16, D), F32)
            for j in range(4):
                total += jnp.where(kind[:, 2 + j : 3 + j] == k, grad_q[pl.ds(pl.multiple_of(j * 256 + t * 16, 16), 16), :], 0.0)
            pair[k, at, :] = total.astype(BF16)
        return carry

    lax.fori_loop(0, 16, pair_rows, 0, unroll=2)
    pair_out = send(pair.at[pl.ds(2 * xp, 2)], pair_p, x_sem.at[2], x_sem.at[3], other_x, r)

    grad_head = mm_nt(pair[0], rel[0])
    for k in range(1, 4):
        grad_head += mm_nt(pair[k], rel[k])
    grad_head = grad_head.astype(BF16)
    for t in range(4):
        q = iota((256, 256), 0) + t * 256
        whole = mm(hot(q - (q >> 3 & 1) * 8 == place_row), grad_head)
        back_s[t * 256 : (t + 1) * 256] = jnp.where(first_half, whole[:, :256], whole[:, 256:]).astype(BF16)
    to_all(rows16(back_s), back_r.at[mine], a2a_sem.at[4], a2a_sem.at[5])
    back_r[mine] = back_s[mine]

    head_out.wait_recv()
    pair_out.wait_recv()
    for k in range(2):
        rel_f[k] = mm(head_t[...], pair[2 * xl + k]) + mm(head_p[...], pair_p[k])
        rel_s[k] = rel_f[k].astype(BF16)
    y_out = []
    for d in range(1, NY):
        yp = lax.rem(y + d, NY)
        part = rel_s.at[:, pl.ds(pl.multiple_of(yp * 128, 128), 128), :]
        y_out.append(send(part, rel_y.at[d - 1], y_sem.at[d - 1], y_sem.at[2 + d], b - y + yp, r))

    for j in range(4):
        onto = hot(iota((D, 256), 0) == rows[6 + j : 7 + j, :])
        high, low = two_parts(pos_w[j * 256 : (j + 1) * 256, 0:1] * query[j * 256 : (j + 1) * 256, :].astype(F32))
        part = mm(onto, high) + mm(onto, low)
        for c in range(4):
            loc[c] = part[:, c * 128 : (c + 1) * 128] if j == 0 else loc[c] + part[:, c * 128 : (c + 1) * 128]

    term_f[...] = jnp.zeros_like(term_f)
    for n in range(1, STOPS):
        term_out[n - 1].wait_recv()

        def own(n=n):
            term_own[...] += term_r[n - 1].astype(F32)

        def other(n=n):
            term_f[0 if OFFS[n] > 0 else 1] += term_r[n - 1].astype(F32)

        pl.when((y + OFFS[n] >= 0) & (y + OFFS[n] < NY))(own)
        pl.when((y + OFFS[n] < 0) | (y + OFFS[n] >= NY))(other)
    relay_s[...] = term_f[...].astype(BF16)
    low_out = remote(relay_s.at[0], relay_r.at[0], hop_sem.at[4], hop_sem.at[5], plane_down, r)
    high_out = remote(relay_s.at[1], relay_r.at[1], hop_sem.at[6], hop_sem.at[7], plane_up, r)
    pl.when(y >= 1)(low_out.start)
    pl.when(y <= 1)(high_out.start)

    wait_all(back_r.at[pl.ds(0, (NBLK - 1) * 16)], a2a_sem.at[5])
    lanes = iota((D, 1024), 1)
    for h in range(2):
        onto = hot((iota((D, 1024), 0) == w_row[0:1, :]) & ((lanes >> 3 & 1) == h))
        part = mm(onto, back_r[...])
        for c in range(2):
            loc[2 * h + c] += part[:, c * 128 : (c + 1) * 128]

    rz_f[...] = rel_f[:, pl.ds(pl.multiple_of(y * 128, 128), 128), :]
    for d in range(1, NY):
        y_out[d - 1].wait_recv()
        rz_f[...] += rel_y[d - 1].astype(F32)
    rz_s[...] = rz_f[...].astype(BF16)
    z_out = []
    for d in range(1, NZ):
        zp = lax.rem(z + d, NZ)
        part = rz_s.at[:, pl.ds(pl.multiple_of(zp * 16, 16), 16), :]
        z_out.append(send(part, rz_r.at[d - 1], z_sem.at[d - 1], z_sem.at[6 + d], b + (zp - z) * NY, r))

    def from_above():
        low_out.wait_recv()
        term_own[...] += relay_r[0].astype(F32)

    def from_below():
        high_out.wait_recv()
        term_own[...] += relay_r[1].astype(F32)

    pl.when(y >= 1)(from_above)
    pl.when(y <= 1)(from_below)
    onto = hot(iota((D, 256), 0) == rows[10:11, :])
    high, low = two_parts(term_own[...])
    part = mm(onto, high) + mm(onto, low)
    for c in range(4):
        loc[c] += part[:, c * 128 : (c + 1) * 128]
        loc_s[c] = loc[c].astype(BF16)
    rep_out = []
    for d in range(1, NREP):
        rp = lax.rem(r + d, NREP)
        rep_out.append(send(loc_s.at[rp], loc_r.at[d - 1], rep_sem.at[d - 1], rep_sem.at[2 + d], b, rp))

    total = rz_f[:, pl.ds(pl.multiple_of(z * 16, 16), 16), :]
    for d in range(1, NZ):
        z_out[d - 1].wait_recv()
        total += rz_r[d - 1].astype(F32)
    for x in range(NX):
        rx_s[x] = total[:, x * 8 : (x + 1) * 8, :]
    x_out = send(rx_s.at[xp], rx_r, x_sem.at[4], x_sem.at[5], other_x, r)
    total = loc[r]
    for d in range(1, NREP):
        rep_out[d - 1].wait_recv()
        total += loc_r[d - 1].astype(F32)
    out_e[...] = total

    for k in range(2):
        out_r[2 * xl + k] = rx_s[xl, k]
    x_out.wait_recv()
    for k in range(2):
        out_r[2 * xp + k] = rx_r[k]

    pl.when(y >= 1)(up_out.wait_send)
    pl.when(y <= 1)(down_out.wait_send)
    pl.when(y >= 1)(low_out.wait_send)
    pl.when(y <= 1)(high_out.wait_send)
    for copy in (*block_out, head_out, *term_out, pair_out, *y_out, *rep_out, *z_out, x_out):
        copy.wait_send()
    wait_all(asked.at[pl.ds(0, NBLK - 1)], a2a_sem.at[0])
    wait_all(served.at[pl.ds(0, (NBLK - 1) * 16)], a2a_sem.at[2])
    wait_all(back_s.at[pl.ds(0, (NBLK - 1) * 16)], a2a_sem.at[4])


def per_device(entity, relation, head_owner, head_row, query_rel, tail_row, neg_row):
    vmem = pl.BlockSpec(memory_space=pltpu.VMEM)
    dma = pltpu.SemaphoreType.DMA
    scratch = [
        pltpu.VMEM((D, D), BF16),
        pltpu.VMEM((4, D, D), BF16),
        pltpu.VMEM((1, 256), I32),
        pltpu.VMEM((1, 256), I32),
        pltpu.VMEM((4, 256), I32),
        pltpu.VMEM((4, 256), I32),
        pltpu.VMEM((1, 256), I32),
        pltpu.VMEM((128, 256), I32),
        pltpu.VMEM((256, 128), I32),
        pltpu.VMEM((NBLK, 1, 128), F32),
        pltpu.VMEM((NBLK, 1, 128), F32),
        pltpu.VMEM((NBLK, 128), F32),
        pltpu.VMEM((8, 1024), I32),
        pltpu.VMEM((1024, 256), BF16),
        pltpu.VMEM((1024, 256), BF16),
        pltpu.VMEM((STOPS * 256, D), BF16),
        pltpu.VMEM((2, 256, D), BF16),
        pltpu.VMEM((1024, D), BF16),
        pltpu.VMEM((256, D), BF16),
        pltpu.VMEM((D, 256), BF16),
        pltpu.VMEM((D, 256), BF16),
        pltpu.VMEM((4, 256, D), F32),
        pltpu.VMEM((1024, D), BF16),
        pltpu.VMEM((1024, 128), F32),
        pltpu.VMEM((1024, D), F32),
        pltpu.VMEM((1024, STOPS * 256), BF16),
        pltpu.VMEM((4, 256, D), BF16),
        pltpu.VMEM((2, 256, D), BF16),
        pltpu.VMEM((256, D), F32),
        pltpu.VMEM((STOPS - 1, 256, D), BF16),
        pltpu.VMEM((STOPS - 1, 256, D), BF16),
        pltpu.VMEM((2, 256, D), F32),
        pltpu.VMEM((2, 256, D), BF16),
        pltpu.VMEM((2, 256, D), BF16),
        pltpu.VMEM((1024, 256), BF16),
        pltpu.VMEM((1024, 256), BF16),
        pltpu.VMEM((2, D, D), F32),
        pltpu.VMEM((2, D, D), BF16),
        pltpu.VMEM((NY - 1, 2, 128, D), BF16),
        pltpu.VMEM((2, 128, D), F32),
        pltpu.VMEM((2, 128, D), BF16),
        pltpu.VMEM((NZ - 1, 2, 16, D), BF16),
        pltpu.VMEM((NX, 2, 8, D), F32),
        pltpu.VMEM((2, 8, D), F32),
        pltpu.VMEM((4, D, 128), F32),
        pltpu.VMEM((4, D, 128), BF16),
        pltpu.VMEM((NREP - 1, D, 128), BF16),
        dma((7,)),
        dma((6,)),
        dma((10,)),
        dma((10,)),
        dma((8,)),
        dma((6,)),
        dma((6,)),
        dma((14,)),
        dma((6,)),
    ]
    return pl.pallas_call(
        kernel,
        out_shape=(jax.ShapeDtypeStruct((D, 128), F32), jax.ShapeDtypeStruct((4, 8, D), F32)),
        in_specs=[pl.BlockSpec(memory_space=pl.ANY)] * 7,
        out_specs=(vmem, vmem),
        scratch_shapes=scratch,
        compiler_params=pltpu.CompilerParams(
            collective_id=0, has_side_effects=True, vmem_limit_bytes=61 * 2**20
        ),
        name="rescal_step",
    )(entity, relation, head_owner.T, head_row[None, :], query_rel.T, tail_row.T, neg_row)


def solution(mesh):
    placed = (
        P("blk", None),
        P("rep", None, None),
        P(("blk", "rep"), None),
        P(("blk", "rep")),
        P(("blk", "rep"), None),
        P(("blk", "rep"), None),
        P("blk", "rep"),
    )
    return jax.shard_map(
        per_device,
        mesh=mesh,
        in_specs=placed,
        out_specs=(P("blk", "rep"), P("rep", "blk", None)),
        check_vma=False,
    )
```

```python
import functools

import jax
import jax.numpy as jnp
from jax import lax
from jax.experimental import pallas as pl
from jax.experimental.pallas import tpu as pltpu
from jax.sharding import PartitionSpec as P

D = 512
STOPS = 6
NBLK, NY, NZ, NX, NREP = 64, 4, 8, 2, 4
OFFS = (0, 1, -1, 2, -2, 3)
MESH = pl.DeviceIdType.MESH
F32, BF16, I32 = jnp.float32, jnp.bfloat16, jnp.int32
NT = (((1,), (1,)), ((), ()))
TN = (((0,), (0,)), ((), ()))


def iota(shape, dim):
    return lax.broadcasted_iota(I32, shape, dim)


def hot(mask):
    return jnp.where(mask, 1.0, 0.0).astype(BF16)


def mm(a, b):
    return jnp.dot(a, b, preferred_element_type=F32)


def mm_nt(a, b):
    return lax.dot_general(a, b, NT, preferred_element_type=F32)


def mm_tn(a, b):
    return lax.dot_general(a, b, TN, preferred_element_type=F32)


def two_parts(value):
    high = value.astype(BF16)
    return high, (value - high.astype(F32)).astype(BF16)


def kernel(
    ent_h, rel_h, owner_h, row_h, kind_h, tail_h, neg_h, out_e, out_r,
    ent, rel, owner_v, row_v, kind_v, tail_v, neg_v, rows, cols, asked, wanted, wanted2, w_row, served, fetched, blocks, relay, tails, head, head_t, head_p,
    prod, query, pos_w, grad_q, weights, pair, pair_p, term_own, term_s, term_r, term_f, relay_s, relay_r, back_s, back_r,
    rel_f, rel_s, rel_y, rel_z, ya_f, ya_s, ya_r, zb_f, zb_s, zb_r, rx_s, rx_r, loc, loc_s, loc_r,
    in_sem, a2a_sem, nb_sem, gt_sem, hop_sem, x_sem, y_sem, z_sem, y2_sem, z2_sem, rep_sem,
):
    b, r = lax.axis_index("blk"), lax.axis_index("rep")
    y, z, xl = lax.rem(b, NY), lax.rem(lax.div(b, NY), NZ), lax.div(b, NY * NZ)
    xp = 1 - xl
    other_x = lax.rem(b + NY * NZ, NBLK)

    def remote(src, dst, s_sem, r_sem, blk, rep):
        return pltpu.make_async_remote_copy(
            src_ref=src, dst_ref=dst, send_sem=s_sem, recv_sem=r_sem, device_id=(blk, rep), device_id_type=MESH
        )

    def send(*copy_args):
        copy = remote(*copy_args)
        copy.start()
        return copy

    def block(n):
        return blocks.at[pl.ds(n * 256, 256)]

    def wait_all(ref, sem):
        pltpu.make_async_copy(ref, ref, sem).wait()

    def to_all(src, dst, s_sem, r_sem):
        def step(k, carry):
            peer = lax.rem(b + k, NBLK)
            send(src(peer), dst, s_sem, r_sem, peer, r)
            return carry

        lax.fori_loop(1, NBLK, step, 0)

    def rows16(ref):
        return lambda s: ref.at[pl.ds(pl.multiple_of(s * 16, 16), 16)]

    barrier = pltpu.get_barrier_semaphore()

    def greet(k, carry):
        pl.semaphore_signal(barrier, inc=1, device_id=(lax.rem(b + k, NBLK), r), device_id_type=MESH)
        return carry

    lax.fori_loop(1, NBLK, greet, 0)
    for d in range(1, NREP):
        pl.semaphore_signal(barrier, inc=1, device_id=(b, lax.rem(r + d, NREP)), device_id_type=MESH)

    index_in = []
    for n, (src, dst) in enumerate(
        ((owner_h, owner_v), (row_h, row_v), (kind_h, kind_v), (tail_h, tail_v), (neg_h, neg_v))
    ):
        index_in.append(pltpu.make_async_copy(src, dst, in_sem.at[n]))
    ent_in = pltpu.make_async_copy(ent_h, ent, in_sem.at[5])
    rel_in = pltpu.make_async_copy(rel_h, rel, in_sem.at[6])
    for copy in (*index_in, ent_in, rel_in):
        copy.start()
    for copy in index_in:
        copy.wait()
    rows[...] = jnp.zeros_like(rows)
    rows[0:1, :] = owner_v[...]
    rows[1:2, :] = row_v[...]
    rows[2:6, :] = kind_v[...]
    rows[6:10, :] = tail_v[...]
    rows[10:11, :] = neg_v[...]
    cols[...] = jnp.transpose(rows[...])

    owner_row, owner_col = rows[0:1, :], cols[:, 0:1]
    in_shard = iota((NBLK, 256), 0) == owner_row
    shard_hot = hot(in_shard)
    before = mm(shard_hot, hot(iota((256, 256), 0) < iota((256, 256), 1)))
    slot_row = jnp.sum(jnp.where(in_shard, before, 0.0), axis=0, keepdims=True)
    place_row = owner_row * 16 + slot_row.astype(I32)
    of_head = iota((256, 128), 1) == owner_col
    before = mm(hot(iota((256, 256), 1) < iota((256, 256), 0)), hot(of_head))
    slot_col = jnp.sum(jnp.where(of_head, before, 0.0), axis=1, keepdims=True).astype(I32)
    place_col = owner_col * 16 + slot_col
    named = cols[:, 1:2] + 1
    lane = iota((256, 128), 1)
    digits = jnp.where(lane == slot_col, named >> 5, 0) + jnp.where(lane == slot_col + 64, named & 31, 0)
    requests = mm(shard_hot, digits.astype(F32).astype(BF16))
    for s in range(NBLK):
        asked[s] = requests[s : s + 1, :]
    ent_in.wait()
    block(0)[...] = mm(hot(iota((256, D), 1) == cols[:, 10:11]), ent[...]).astype(BF16)
    rel_in.wait()

    pl.semaphore_wait(barrier, NBLK - 1 + NREP - 1)
    to_all(lambda s: asked.at[s], wanted.at[b], a2a_sem.at[0], a2a_sem.at[1])
    wanted[b] = asked[b]

    plane_up, plane_down = lax.rem(b + NY, NBLK), lax.rem(b + NBLK - NY, NBLK)
    up_out = remote(block(0), relay.at[0], hop_sem.at[0], hop_sem.at[1], plane_up, r)
    down_out = remote(block(0), relay.at[1], hop_sem.at[2], hop_sem.at[3], plane_down, r)
    pl.when(y >= 1)(up_out.start)
    pl.when(y <= 1)(down_out.start)
    block_out, block_far = [], []
    for n in range(1, STOPS):
        visitor = b - y + lax.rem(y + OFFS[n] + NY, NY)
        sems = nb_sem.at[n - 1], nb_sem.at[4 + n]
        block_out.append(remote(block(0), block(n), *sems, visitor, r))
        block_far.append(remote(relay.at[0 if OFFS[n] > 0 else 1], block(n), *sems, visitor, r))
        pl.when((y + OFFS[n] >= 0) & (y + OFFS[n] < NY))(block_out[n - 1].start)
    for j in range(2):
        tails[j * 256 : (j + 1) * 256] = mm(hot(iota((256, D), 1) == cols[:, 6 + j : 7 + j]), ent[...]).astype(BF16)
    wait_all(wanted.at[pl.ds(0, NBLK - 1)], a2a_sem.at[1])

    for s in range(NBLK):
        wanted2[s : s + 1, :] = wanted[s]
    spread = mm(hot(iota((1024, NBLK), 0) >> 4 == iota((1024, NBLK), 1)), wanted2[...].astype(BF16))
    k_of, lane = iota((1024, 128), 0) & 7, iota((1024, 128), 1)
    spread = jnp.where(lane == k_of, spread * 32.0, jnp.where(lane == k_of + 64, spread, 0.0))
    w_row[...] = mm_nt(jnp.ones((8, 128), BF16), spread.astype(BF16)).astype(I32) - 1
    w_col = jnp.sum(spread, axis=1, keepdims=True).astype(I32) - 1
    first_half = (iota((256, 256), 0) >> 3 & 1) == 0
    for t in range(4):
        whole = mm(hot(iota((256, D), 1) == w_col[t * 256 : (t + 1) * 256]), ent[...])
        served[t * 256 : (t + 1) * 256] = jnp.where(first_half, whole[:, :256], whole[:, 256:]).astype(BF16)
    mine = pl.ds(pl.multiple_of(b * 16, 16), 16)
    to_all(rows16(served), fetched.at[mine], a2a_sem.at[2], a2a_sem.at[3])
    fetched[mine] = served[mine]
    pl.when(y >= 1)(up_out.wait_recv)
    pl.when(y <= 1)(down_out.wait_recv)
    for n in range(1, STOPS):
        pl.when((y + OFFS[n] < 0) | (y + OFFS[n] >= NY))(block_far[n - 1].start)
    for j in range(2, 4):
        tails[j * 256 : (j + 1) * 256] = mm(hot(iota((256, D), 1) == cols[:, 6 + j : 7 + j]), ent[...]).astype(BF16)
    wait_all(fetched.at[pl.ds(0, (NBLK - 1) * 16)], a2a_sem.at[3])
    for h in range(2):
        picked = hot(iota((256, 1024), 1) == place_col + 8 * h)
        head[:, h * 256 : (h + 1) * 256] = mm(picked, fetched[...]).astype(BF16)

    for k in range(4):
        prod[k] = mm(head[...], rel[k])

    def query_rows(t, carry):
        at = pl.ds(pl.multiple_of(t * 16, 16), 16)
        kind = cols[at, :]
        for j in range(4):
            to = pl.ds(pl.multiple_of(j * 256 + t * 16, 16), 16)
            q = prod[0, at, :]
            for k in range(1, 4):
                q = jnp.where(kind[:, 2 + j : 3 + j] == k, prod[k, at, :], q)
            q = q.astype(BF16)
            query[to, :] = q
            tail = tails[to, :].astype(F32)
            score = jnp.sum(q.astype(F32) * tail, axis=1, keepdims=True)
            weight = jax.nn.sigmoid(score) - 1.0
            grad_q[to, :] = weight * tail
            pos_w[to, :] = jnp.broadcast_to(weight, (16, 128))
        return carry

    lax.fori_loop(0, 16, query_rows, 0, unroll=2)

    c = iota((D, D), 0)
    natural = (c >> 3 & 1) * 256 + (c >> 4 & 7) * 32 + (c >> 7) * 8 + (c & 7)
    head_t[...] = mm_nt(hot(iota((D, D), 1) == natural), head[...]).astype(BF16)
    head_out = send(head_t, head_p, x_sem.at[0], x_sem.at[1], other_x, r)

    term_out = []
    for n in range(STOPS):
        if n:
            block_out[n - 1].wait_recv()
        met = slice(n * 256, (n + 1) * 256)
        weights[:, met] = (jax.nn.sigmoid(mm_nt(query[...], block(n)[...])) * (1.0 / STOPS)).astype(BF16)
        term = mm_tn(weights[:, met], query[...])
        if n == 0:
            term_own[...] = term
        else:
            term_s[n - 1] = term.astype(BF16)
            via = b - y + lax.rem(y - OFFS[n] + NY, NY)
            term_out.append(send(term_s.at[n - 1], term_r.at[n - 1], gt_sem.at[n - 1], gt_sem.at[4 + n], via, r))
        for upto, since in ((4, 0), (STOPS, 4)):
            if n == upto - 1:
                met = slice(since * 256, upto * 256)
                for j in range(4):
                    at = slice(j * 256, (j + 1) * 256)
                    grad_q[at, :] += mm(weights[at, met], blocks[met, :])

    def pair_rows(t, carry):
        at = pl.ds(pl.multiple_of(t * 16, 16), 16)
        kind = cols[at, :]
        for k in range(4):
            total = jnp.zeros((16, D), F32)
            for j in range(4):
                total += jnp.where(kind[:, 2 + j : 3 + j] == k, grad_q[pl.ds(pl.multiple_of(j * 256 + t * 16, 16), 16), :], 0.0)
            pair[k, at, :] = total.astype(BF16)
        return carry

    lax.fori_loop(0, 16, pair_rows, 0, unroll=2)
    pair_out = send(pair.at[pl.ds(2 * xp, 2)], pair_p, x_sem.at[2], x_sem.at[3], other_x, r)

    grad_head = mm_nt(pair[0], rel[0])
    for k in range(1, 4):
        grad_head += mm_nt(pair[k], rel[k])
    grad_head = grad_head.astype(BF16)
    for t in range(4):
        q = iota((256, 256), 0) + t * 256
        whole = mm(hot(q - (q >> 3 & 1) * 8 == place_row), grad_head)
        back_s[t * 256 : (t + 1) * 256] = jnp.where(first_half, whole[:, :256], whole[:, 256:]).astype(BF16)
    to_all(rows16(back_s), back_r.at[mine], a2a_sem.at[4], a2a_sem.at[5])
    back_r[mine] = back_s[mine]

    for j in range(4):
        onto = hot(iota((D, 256), 0) == rows[6 + j : 7 + j, :])
        high, low = two_parts(pos_w[j * 256 : (j + 1) * 256, 0:1] * query[j * 256 : (j + 1) * 256, :].astype(F32))
        part = mm(onto, high) + mm(onto, low)
        for c in range(4):
            loc[c] = part[:, c * 128 : (c + 1) * 128] if j == 0 else loc[c] + part[:, c * 128 : (c + 1) * 128]

    head_out.wait_recv()
    pair_out.wait_recv()
    for k in (1, 0):
        total = (mm(head_t[...], pair[2 * xl + k]) + mm(head_p[...], pair_p[k])).reshape(NY, NZ, 16, D)
        rel_f[k] = total
        rel_s[k] = total.astype(BF16)
        if k:
            zb_in = []
            for d in range(1, NZ):
                zp = lax.rem(z + d, NZ)
                to = b + (zp - z) * NY
                zb_in.append(send(rel_s.at[1, :, zp], rel_z.at[d - 1], z_sem.at[d - 1], z_sem.at[6 + d], to, r))
    ya_in = []
    for d in range(1, NY):
        yp = lax.rem(y + d, NY)
        ya_in.append(send(rel_s.at[0, yp], rel_y.at[d - 1], y_sem.at[d - 1], y_sem.at[2 + d], b - y + yp, r))

    term_f[...] = jnp.zeros_like(term_f)
    for n in range(1, STOPS):
        term_out[n - 1].wait_recv()

        def own(n=n):
            term_own[...] += term_r[n - 1].astype(F32)

        def other(n=n):
            term_f[0 if OFFS[n] > 0 else 1] += term_r[n - 1].astype(F32)

        pl.when((y + OFFS[n] >= 0) & (y + OFFS[n] < NY))(own)
        pl.when((y + OFFS[n] < 0) | (y + OFFS[n] >= NY))(other)
    relay_s[...] = term_f[...].astype(BF16)
    low_out = remote(relay_s.at[0], relay_r.at[0], hop_sem.at[4], hop_sem.at[5], plane_down, r)
    high_out = remote(relay_s.at[1], relay_r.at[1], hop_sem.at[6], hop_sem.at[7], plane_up, r)
    pl.when(y >= 1)(low_out.start)
    pl.when(y <= 1)(high_out.start)

    wait_all(back_r.at[pl.ds(0, (NBLK - 1) * 16)], a2a_sem.at[5])
    lanes = iota((D, 1024), 1)
    for h in range(2):
        onto = hot((iota((D, 1024), 0) == w_row[0:1, :]) & ((lanes >> 3 & 1) == h))
        part = mm(onto, back_r[...])
        for c in range(2):
            loc[2 * h + c] += part[:, c * 128 : (c + 1) * 128]

    total = rel_f[0, y]
    for d in range(1, NY):
        ya_in[d - 1].wait_recv()
        total += rel_y[d - 1].astype(F32)
    ya_f[...] = total
    ya_s[...] = total.astype(BF16)
    ya_out = []
    for d in range(1, NZ):
        zp = lax.rem(z + d, NZ)
        to = b + (zp - z) * NY
        ya_out.append(send(ya_s.at[zp], ya_r.at[d - 1], z2_sem.at[d - 1], z2_sem.at[6 + d], to, r))
    total = rel_f[1, :, z]
    for d in range(1, NZ):
        zb_in[d - 1].wait_recv()
        total += rel_z[d - 1].astype(F32)
    zb_f[...] = total
    zb_s[...] = total.astype(BF16)
    zb_out = []
    for d in range(1, NY):
        yp = lax.rem(y + d, NY)
        zb_out.append(send(zb_s.at[yp], zb_r.at[d - 1], y2_sem.at[d - 1], y2_sem.at[2 + d], b - y + yp, r))

    def from_above():
        low_out.wait_recv()
        term_own[...] += relay_r[0].astype(F32)

    def from_below():
        high_out.wait_recv()
        term_own[...] += relay_r[1].astype(F32)

    pl.when(y >= 1)(from_above)
    pl.when(y <= 1)(from_below)
    onto = hot(iota((D, 256), 0) == rows[10:11, :])
    high, low = two_parts(term_own[...])
    part = mm(onto, high) + mm(onto, low)
    for c in range(4):
        loc[c] += part[:, c * 128 : (c + 1) * 128]
        loc_s[c] = loc[c].astype(BF16)
    rep_out = []
    for d in range(1, NREP):
        rp = lax.rem(r + d, NREP)
        rep_out.append(send(loc_s.at[rp], loc_r.at[d - 1], rep_sem.at[d - 1], rep_sem.at[2 + d], b, rp))

    total = ya_f[z]
    for d in range(1, NZ):
        ya_out[d - 1].wait_recv()
        total += ya_r[d - 1].astype(F32)
    for x in range(NX):
        rx_s[x, 0] = total[x * 8 : (x + 1) * 8, :]
    total = zb_f[y]
    for d in range(1, NY):
        zb_out[d - 1].wait_recv()
        total += zb_r[d - 1].astype(F32)
    for x in range(NX):
        rx_s[x, 1] = total[x * 8 : (x + 1) * 8, :]
    x_out = send(rx_s.at[xp], rx_r, x_sem.at[4], x_sem.at[5], other_x, r)
    total = loc[r]
    for d in range(1, NREP):
        rep_out[d - 1].wait_recv()
        total += loc_r[d - 1].astype(F32)
    out_e[...] = total

    for k in range(2):
        out_r[2 * xl + k] = rx_s[xl, k]
    x_out.wait_recv()
    for k in range(2):
        out_r[2 * xp + k] = rx_r[k]

    pl.when(y >= 1)(up_out.wait_send)
    pl.when(y <= 1)(down_out.wait_send)
    pl.when(y >= 1)(low_out.wait_send)
    pl.when(y <= 1)(high_out.wait_send)
    for copy in (*block_out, head_out, *term_out, pair_out, *ya_in, *zb_in, *ya_out, *zb_out, *rep_out, x_out):
        copy.wait_send()
    wait_all(asked.at[pl.ds(0, NBLK - 1)], a2a_sem.at[0])
    wait_all(served.at[pl.ds(0, (NBLK - 1) * 16)], a2a_sem.at[2])
    wait_all(back_s.at[pl.ds(0, (NBLK - 1) * 16)], a2a_sem.at[4])


def per_device(entity, relation, head_owner, head_row, query_rel, tail_row, neg_row):
    vmem = pl.BlockSpec(memory_space=pltpu.VMEM)
    dma = pltpu.SemaphoreType.DMA
    scratch = [
        pltpu.VMEM((D, D), BF16),
        pltpu.VMEM((4, D, D), BF16),
        pltpu.VMEM((1, 256), I32),
        pltpu.VMEM((1, 256), I32),
        pltpu.VMEM((4, 256), I32),
        pltpu.VMEM((4, 256), I32),
        pltpu.VMEM((1, 256), I32),
        pltpu.VMEM((128, 256), I32),
        pltpu.VMEM((256, 128), I32),
        pltpu.VMEM((NBLK, 1, 128), F32),
        pltpu.VMEM((NBLK, 1, 128), F32),
        pltpu.VMEM((NBLK, 128), F32),
        pltpu.VMEM((8, 1024), I32),
        pltpu.VMEM((1024, 256), BF16),
        pltpu.VMEM((1024, 256), BF16),
        pltpu.VMEM((STOPS * 256, D), BF16),
        pltpu.VMEM((2, 256, D), BF16),
        pltpu.VMEM((1024, D), BF16),
        pltpu.VMEM((256, D), BF16),
        pltpu.VMEM((D, 256), BF16),
        pltpu.VMEM((D, 256), BF16),
        pltpu.VMEM((4, 256, D), F32),
        pltpu.VMEM((1024, D), BF16),
        pltpu.VMEM((1024, 128), F32),
        pltpu.VMEM((1024, D), F32),
        pltpu.VMEM((1024, STOPS * 256), BF16),
        pltpu.VMEM((4, 256, D), BF16),
        pltpu.VMEM((2, 256, D), BF16),
        pltpu.VMEM((256, D), F32),
        pltpu.VMEM((STOPS - 1, 256, D), BF16),
        pltpu.VMEM((STOPS - 1, 256, D), BF16),
        pltpu.VMEM((2, 256, D), F32),
        pltpu.VMEM((2, 256, D), BF16),
        pltpu.VMEM((2, 256, D), BF16),
        pltpu.VMEM((1024, 256), BF16),
        pltpu.VMEM((1024, 256), BF16),
        pltpu.VMEM((2, NY, NZ, 16, D), F32),
        pltpu.VMEM((2, NY, NZ, 16, D), BF16),
        pltpu.VMEM((NY - 1, NZ, 16, D), BF16),
        pltpu.VMEM((NZ - 1, NY, 16, D), BF16),
        pltpu.VMEM((NZ, 16, D), F32),
        pltpu.VMEM((NZ, 16, D), BF16),
        pltpu.VMEM((NZ - 1, 16, D), BF16),
        pltpu.VMEM((NY, 16, D), F32),
        pltpu.VMEM((NY, 16, D), BF16),
        pltpu.VMEM((NY - 1, 16, D), BF16),
        pltpu.VMEM((NX, 2, 8, D), F32),
        pltpu.VMEM((2, 8, D), F32),
        pltpu.VMEM((4, D, 128), F32),
        pltpu.VMEM((4, D, 128), BF16),
        pltpu.VMEM((NREP - 1, D, 128), BF16),
        dma((7,)),
        dma((6,)),
        dma((10,)),
        dma((10,)),
        dma((8,)),
        dma((6,)),
        dma((6,)),
        dma((14,)),
        dma((6,)),
        dma((14,)),
        dma((6,)),
    ]
    return pl.pallas_call(
        kernel,
        out_shape=(jax.ShapeDtypeStruct((D, 128), F32), jax.ShapeDtypeStruct((4, 8, D), F32)),
        in_specs=[pl.BlockSpec(memory_space=pl.ANY)] * 7,
        out_specs=(vmem, vmem),
        scratch_shapes=scratch,
        compiler_params=pltpu.CompilerParams(
            collective_id=0, has_side_effects=True, vmem_limit_bytes=61 * 2**20
        ),
        name="rescal_step",
    )(entity, relation, head_owner.T, head_row[None, :], query_rel.T, tail_row.T, neg_row)


def solution(mesh):
    placed = (
        P("blk", None),
        P("rep", None, None),
        P(("blk", "rep"), None),
        P(("blk", "rep")),
        P(("blk", "rep"), None),
        P(("blk", "rep"), None),
        P("blk", "rep"),
    )
    return jax.shard_map(
        per_device,
        mesh=mesh,
        in_specs=placed,
        out_specs=(P("blk", "rep"), P("rep", "blk", None)),
        check_vma=False,
    )
```

```python
import functools

import jax
import jax.numpy as jnp
from jax import lax
from jax.experimental import pallas as pl
from jax.experimental.pallas import tpu as pltpu
from jax.sharding import PartitionSpec as P

D = 512
STOPS = 6
NBLK, NY, NZ, NX, NREP = 64, 4, 8, 2, 4
OFFS = (0, 1, -1, 2, -2, 3)
MESH = pl.DeviceIdType.MESH
F32, BF16, I32 = jnp.float32, jnp.bfloat16, jnp.int32
NT = (((1,), (1,)), ((), ()))
TN = (((0,), (0,)), ((), ()))


def iota(shape, dim):
    return lax.broadcasted_iota(I32, shape, dim)


def hot(mask):
    return jnp.where(mask, 1.0, 0.0).astype(BF16)


def mm(a, b):
    return jnp.dot(a, b, preferred_element_type=F32)


def mm_nt(a, b):
    return lax.dot_general(a, b, NT, preferred_element_type=F32)


def mm_tn(a, b):
    return lax.dot_general(a, b, TN, preferred_element_type=F32)


def two_parts(value):
    high = value.astype(BF16)
    return high, (value - high.astype(F32)).astype(BF16)


def kernel(
    ent_h, rel_h, owner_h, row_h, kind_h, tail_h, neg_h, out_e, out_r,
    ent, rel, owner_v, row_v, kind_v, tail_v, neg_v, rows, cols, asked, wanted, wanted2, w_row, served, fetched, blocks, relay, tails, head, head_t, head_p,
    prod, query, pos_w, grad_q, weights, pair, pair_p, term_own, term_s, term_r, near, chain_r, term_f, relay_s, relay_r, back_s, back_r,
    rel_f, rel_s, rel_y, rz_f, rz_s, rz_r, rx_s, rx_r, loc, loc_s, loc_r,
    in_sem, a2a_sem, nb_sem, gt_sem, chain_sem, hop_sem, x_sem, y_sem, z_sem, rep_sem,
):
    b, r = lax.axis_index("blk"), lax.axis_index("rep")
    y, z, xl = lax.rem(b, NY), lax.rem(lax.div(b, NY), NZ), lax.div(b, NY * NZ)
    xp = 1 - xl
    other_x = lax.rem(b + NY * NZ, NBLK)

    def remote(src, dst, s_sem, r_sem, blk, rep):
        return pltpu.make_async_remote_copy(
            src_ref=src, dst_ref=dst, send_sem=s_sem, recv_sem=r_sem, device_id=(blk, rep), device_id_type=MESH
        )

    def send(*copy_args):
        copy = remote(*copy_args)
        copy.start()
        return copy

    def block(n):
        return blocks.at[pl.ds(n * 256, 256)]

    def wait_all(ref, sem):
        pltpu.make_async_copy(ref, ref, sem).wait()

    def to_all(src, dst, s_sem, r_sem):
        def step(k, carry):
            peer = lax.rem(b + k, NBLK)
            send(src(peer), dst, s_sem, r_sem, peer, r)
            return carry

        lax.fori_loop(1, NBLK, step, 0)

    def rows16(ref):
        return lambda s: ref.at[pl.ds(pl.multiple_of(s * 16, 16), 16)]

    barrier = pltpu.get_barrier_semaphore()

    def greet(k, carry):
        pl.semaphore_signal(barrier, inc=1, device_id=(lax.rem(b + k, NBLK), r), device_id_type=MESH)
        return carry

    lax.fori_loop(1, NBLK, greet, 0)
    for d in range(1, NREP):
        pl.semaphore_signal(barrier, inc=1, device_id=(b, lax.rem(r + d, NREP)), device_id_type=MESH)

    index_in = []
    for n, (src, dst) in enumerate(
        ((owner_h, owner_v), (row_h, row_v), (kind_h, kind_v), (tail_h, tail_v), (neg_h, neg_v))
    ):
        index_in.append(pltpu.make_async_copy(src, dst, in_sem.at[n]))
    ent_in = pltpu.make_async_copy(ent_h, ent, in_sem.at[5])
    rel_in = pltpu.make_async_copy(rel_h, rel, in_sem.at[6])
    for copy in (*index_in, ent_in, rel_in):
        copy.start()
    for copy in index_in:
        copy.wait()
    rows[...] = jnp.zeros_like(rows)
    rows[0:1, :] = owner_v[...]
    rows[1:2, :] = row_v[...]
    rows[2:6, :] = kind_v[...]
    rows[6:10, :] = tail_v[...]
    rows[10:11, :] = neg_v[...]
    cols[...] = jnp.transpose(rows[...])

    owner_row, owner_col = rows[0:1, :], cols[:, 0:1]
    in_shard = iota((NBLK, 256), 0) == owner_row
    shard_hot = hot(in_shard)
    before = mm(shard_hot, hot(iota((256, 256), 0) < iota((256, 256), 1)))
    slot_row = jnp.sum(jnp.where(in_shard, before, 0.0), axis=0, keepdims=True)
    place_row = owner_row * 16 + slot_row.astype(I32)
    of_head = iota((256, 128), 1) == owner_col
    before = mm(hot(iota((256, 256), 1) < iota((256, 256), 0)), hot(of_head))
    slot_col = jnp.sum(jnp.where(of_head, before, 0.0), axis=1, keepdims=True).astype(I32)
    place_col = owner_col * 16 + slot_col
    named = cols[:, 1:2] + 1
    lane = iota((256, 128), 1)
    digits = jnp.where(lane == slot_col, named >> 5, 0) + jnp.where(lane == slot_col + 64, named & 31, 0)
    requests = mm(shard_hot, digits.astype(F32).astype(BF16))
    for s in range(NBLK):
        asked[s] = requests[s : s + 1, :]
    ent_in.wait()
    block(0)[...] = mm(hot(iota((256, D), 1) == cols[:, 10:11]), ent[...]).astype(BF16)
    rel_in.wait()

    pl.semaphore_wait(barrier, NBLK - 1 + NREP - 1)
    to_all(lambda s: asked.at[s], wanted.at[b], a2a_sem.at[0], a2a_sem.at[1])
    wanted[b] = asked[b]

    plane_up, plane_down = lax.rem(b + NY, NBLK), lax.rem(b + NBLK - NY, NBLK)
    up_out = remote(block(0), relay.at[0], hop_sem.at[0], hop_sem.at[1], plane_up, r)
    down_out = remote(block(0), relay.at[1], hop_sem.at[2], hop_sem.at[3], plane_down, r)
    pl.when(y >= 1)(up_out.start)
    pl.when(y <= 1)(down_out.start)
    block_out, block_far = [], []
    for n in range(1, STOPS):
        visitor = b - y + lax.rem(y + OFFS[n] + NY, NY)
        sems = nb_sem.at[n - 1], nb_sem.at[4 + n]
        block_out.append(remote(block(0), block(n), *sems, visitor, r))
        block_far.append(remote(relay.at[0 if OFFS[n] > 0 else 1], block(n), *sems, visitor, r))
        if abs(OFFS[n]) != 2:
            pl.when((y + OFFS[n] >= 0) & (y + OFFS[n] < NY))(block_out[n - 1].start)
    for j in range(2):
        tails[j * 256 : (j + 1) * 256] = mm(hot(iota((256, D), 1) == cols[:, 6 + j : 7 + j]), ent[...]).astype(BF16)
    wait_all(wanted.at[pl.ds(0, NBLK - 1)], a2a_sem.at[1])

    for s in range(NBLK):
        wanted2[s : s + 1, :] = wanted[s]
    spread = mm(hot(iota((1024, NBLK), 0) >> 4 == iota((1024, NBLK), 1)), wanted2[...].astype(BF16))
    k_of, lane = iota((1024, 128), 0) & 7, iota((1024, 128), 1)
    spread = jnp.where(lane == k_of, spread * 32.0, jnp.where(lane == k_of + 64, spread, 0.0))
    w_row[...] = mm_nt(jnp.ones((8, 128), BF16), spread.astype(BF16)).astype(I32) - 1
    w_col = jnp.sum(spread, axis=1, keepdims=True).astype(I32) - 1
    first_half = (iota((256, 256), 0) >> 3 & 1) == 0
    for t in range(4):
        whole = mm(hot(iota((256, D), 1) == w_col[t * 256 : (t + 1) * 256]), ent[...])
        served[t * 256 : (t + 1) * 256] = jnp.where(first_half, whole[:, :256], whole[:, 256:]).astype(BF16)
    mine = pl.ds(pl.multiple_of(b * 16, 16), 16)
    to_all(rows16(served), fetched.at[mine], a2a_sem.at[2], a2a_sem.at[3])
    fetched[mine] = served[mine]
    pl.when(y >= 1)(up_out.wait_recv)
    pl.when(y <= 1)(down_out.wait_recv)
    for n in (1, 2, 5):
        pl.when((y + OFFS[n] < 0) | (y + OFFS[n] >= NY))(block_far[n - 1].start)
    pl.when(y == 2)(block_far[2].start)
    pl.when(y == 1)(block_far[3].start)
    next_y, last_y = b - y + lax.rem(y + 1, NY), b - y + lax.rem(y + NY - 1, NY)
    on_up = remote(block(1), block(3), chain_sem.at[0], nb_sem.at[7], next_y, r)
    on_down = remote(block(2), block(4), chain_sem.at[1], nb_sem.at[8], last_y, r)
    block_out[0].wait_recv()
    pl.when(y <= 2)(on_up.start)
    block_out[1].wait_recv()
    pl.when(y >= 1)(on_down.start)
    for j in range(2, 4):
        tails[j * 256 : (j + 1) * 256] = mm(hot(iota((256, D), 1) == cols[:, 6 + j : 7 + j]), ent[...]).astype(BF16)
    wait_all(fetched.at[pl.ds(0, (NBLK - 1) * 16)], a2a_sem.at[3])
    for h in range(2):
        picked = hot(iota((256, 1024), 1) == place_col + 8 * h)
        head[:, h * 256 : (h + 1) * 256] = mm(picked, fetched[...]).astype(BF16)

    for k in range(4):
        prod[k] = mm(head[...], rel[k])

    def query_rows(t, carry):
        at = pl.ds(pl.multiple_of(t * 16, 16), 16)
        kind = cols[at, :]
        for j in range(4):
            to = pl.ds(pl.multiple_of(j * 256 + t * 16, 16), 16)
            q = prod[0, at, :]
            for k in range(1, 4):
                q = jnp.where(kind[:, 2 + j : 3 + j] == k, prod[k, at, :], q)
            q = q.astype(BF16)
            query[to, :] = q
            tail = tails[to, :].astype(F32)
            score = jnp.sum(q.astype(F32) * tail, axis=1, keepdims=True)
            weight = jax.nn.sigmoid(score) - 1.0
            grad_q[to, :] = weight * tail
            pos_w[to, :] = jnp.broadcast_to(weight, (16, 128))
        return carry

    lax.fori_loop(0, 16, query_rows, 0, unroll=2)

    c = iota((D, D), 0)
    natural = (c >> 3 & 1) * 256 + (c >> 4 & 7) * 32 + (c >> 7) * 8 + (c & 7)
    head_t[...] = mm_nt(hot(iota((D, D), 1) == natural), head[...]).astype(BF16)
    head_out = send(head_t, head_p, x_sem.at[0], x_sem.at[1], other_x, r)

    term_out = []
    for n in range(STOPS):
        if n > 2:
            block_out[n - 1].wait_recv()
        met = slice(n * 256, (n + 1) * 256)
        weights[:, met] = (jax.nn.sigmoid(mm_nt(query[...], block(n)[...])) * (1.0 / STOPS)).astype(BF16)
        term = mm_tn(weights[:, met], query[...])
        if n == 0:
            term_own[...] = term
        else:
            via = b - y + lax.rem(y - OFFS[n] + NY, NY)
            term_out.append(remote(term_s.at[n - 1], term_r.at[n - 1], gt_sem.at[n - 1], gt_sem.at[4 + n], via, r))
            if n <= 2:
                near[n - 1] = term
                continue
            term_s[n - 1] = term.astype(BF16)
            if n == 3:
                pl.when(y == 0)(term_out[2].start)
                term_up = remote(term_s.at[2], chain_r.at[0], gt_sem.at[2], chain_sem.at[2], last_y, r)
                pl.when(y >= 1)(term_up.start)
            elif n == 4:
                pl.when(y == 3)(term_out[3].start)
                term_down = remote(term_s.at[3], chain_r.at[1], gt_sem.at[3], chain_sem.at[3], next_y, r)
                pl.when(y <= 2)(term_down.start)
            else:
                term_out[4].start()
        for upto, since in ((4, 0), (STOPS, 4)):
            if n == upto - 1:
                met = slice(since * 256, upto * 256)
                for j in range(4):
                    at = slice(j * 256, (j + 1) * 256)
                    grad_q[at, :] += mm(weights[at, met], blocks[met, :])

    def pair_rows(t, carry):
        at = pl.ds(pl.multiple_of(t * 16, 16), 16)
        kind = cols[at, :]
        for k in range(4):
            total = jnp.zeros((16, D), F32)
            for j in range(4):
                total += jnp.where(kind[:, 2 + j : 3 + j] == k, grad_q[pl.ds(pl.multiple_of(j * 256 + t * 16, 16), 16), :], 0.0)
            pair[k, at, :] = total.astype(BF16)
        return carry

    lax.fori_loop(0, 16, pair_rows, 0, unroll=2)
    pair_out = send(pair.at[pl.ds(2 * xp, 2)], pair_p, x_sem.at[2], x_sem.at[3], other_x, r)

    grad_head = mm_nt(pair[0], rel[0])
    for k in range(1, 4):
        grad_head += mm_nt(pair[k], rel[k])
    grad_head = grad_head.astype(BF16)
    for t in range(4):
        q = iota((256, 256), 0) + t * 256
        whole = mm(hot(q - (q >> 3 & 1) * 8 == place_row), grad_head)
        back_s[t * 256 : (t + 1) * 256] = jnp.where(first_half, whole[:, :256], whole[:, 256:]).astype(BF16)
    to_all(rows16(back_s), back_r.at[mine], a2a_sem.at[4], a2a_sem.at[5])
    back_r[mine] = back_s[mine]

    for j in range(4):
        onto = hot(iota((D, 256), 0) == rows[6 + j : 7 + j, :])
        high, low = two_parts(pos_w[j * 256 : (j + 1) * 256, 0:1] * query[j * 256 : (j + 1) * 256, :].astype(F32))
        part = mm(onto, high) + mm(onto, low)
        for c in range(4):
            loc[c] = part[:, c * 128 : (c + 1) * 128] if j == 0 else loc[c] + part[:, c * 128 : (c + 1) * 128]

    def add_up():
        term_up.wait_recv()
        near[0] += chain_r[0].astype(F32)

    def add_down():
        term_down.wait_recv()
        near[1] += chain_r[1].astype(F32)

    pl.when(y <= 2)(add_up)
    pl.when(y >= 1)(add_down)
    for n in (1, 2):
        term_s[n - 1] = near[n - 1].astype(BF16)
        term_out[n - 1].start()

    head_out.wait_recv()
    pair_out.wait_recv()
    for k in range(2):
        rel_f[k] = mm(head_t[...], pair[2 * xl + k]) + mm(head_p[...], pair_p[k])
        rel_s[k] = rel_f[k].astype(BF16)
    y_out = []
    for d in range(1, NY):
        yp = lax.rem(y + d, NY)
        part = rel_s.at[:, pl.ds(pl.multiple_of(yp * 128, 128), 128), :]
        y_out.append(send(part, rel_y.at[d - 1], y_sem.at[d - 1], y_sem.at[2 + d], b - y + yp, r))

    term_f[...] = jnp.zeros_like(term_f)
    for n in range(1, STOPS):

        def own(n=n):
            term_own[...] += term_r[n - 1].astype(F32)

        def other(n=n):
            term_f[0 if OFFS[n] > 0 else 1] += term_r[n - 1].astype(F32)

        def far(n=n):
            term_out[n - 1].wait_recv()
            term_f[0 if OFFS[n] > 0 else 1] += term_r[n - 1].astype(F32)

        if n == 3:
            pl.when(y == 2)(far)
        elif n == 4:
            pl.when(y == 1)(far)
        else:
            term_out[n - 1].wait_recv()
            pl.when((y + OFFS[n] >= 0) & (y + OFFS[n] < NY))(own)
            pl.when((y + OFFS[n] < 0) | (y + OFFS[n] >= NY))(other)
    relay_s[...] = term_f[...].astype(BF16)
    low_out = remote(relay_s.at[0], relay_r.at[0], hop_sem.at[4], hop_sem.at[5], plane_down, r)
    high_out = remote(relay_s.at[1], relay_r.at[1], hop_sem.at[6], hop_sem.at[7], plane_up, r)
    pl.when(y >= 1)(low_out.start)
    pl.when(y <= 1)(high_out.start)

    wait_all(back_r.at[pl.ds(0, (NBLK - 1) * 16)], a2a_sem.at[5])
    lanes = iota((D, 1024), 1)
    for h in range(2):
        onto = hot((iota((D, 1024), 0) == w_row[0:1, :]) & ((lanes >> 3 & 1) == h))
        part = mm(onto, back_r[...])
        for c in range(2):
            loc[2 * h + c] += part[:, c * 128 : (c + 1) * 128]

    rz_f[...] = rel_f[:, pl.ds(pl.multiple_of(y * 128, 128), 128), :]
    for d in range(1, NY):
        y_out[d - 1].wait_recv()
        rz_f[...] += rel_y[d - 1].astype(F32)
    rz_s[...] = rz_f[...].astype(BF16)
    z_out = []
    for d in range(1, NZ):
        zp = lax.rem(z + d, NZ)
        part = rz_s.at[:, pl.ds(pl.multiple_of(zp * 16, 16), 16), :]
        z_out.append(send(part, rz_r.at[d - 1], z_sem.at[d - 1], z_sem.at[6 + d], b + (zp - z) * NY, r))

    def from_above():
        low_out.wait_recv()
        term_own[...] += relay_r[0].astype(F32)

    def from_below():
        high_out.wait_recv()
        term_own[...] += relay_r[1].astype(F32)

    pl.when(y >= 1)(from_above)
    pl.when(y <= 1)(from_below)
    onto = hot(iota((D, 256), 0) == rows[10:11, :])
    high, low = two_parts(term_own[...])
    part = mm(onto, high) + mm(onto, low)
    for c in range(4):
        loc[c] += part[:, c * 128 : (c + 1) * 128]
        loc_s[c] = loc[c].astype(BF16)
    rep_out = []
    for d in range(1, NREP):
        rp = lax.rem(r + d, NREP)
        rep_out.append(send(loc_s.at[rp], loc_r.at[d - 1], rep_sem.at[d - 1], rep_sem.at[2 + d], b, rp))

    total = rz_f[:, pl.ds(pl.multiple_of(z * 16, 16), 16), :]
    for d in range(1, NZ):
        z_out[d - 1].wait_recv()
        total += rz_r[d - 1].astype(F32)
    for x in range(NX):
        rx_s[x] = total[:, x * 8 : (x + 1) * 8, :]
    x_out = send(rx_s.at[xp], rx_r, x_sem.at[4], x_sem.at[5], other_x, r)
    total = loc[r]
    for d in range(1, NREP):
        rep_out[d - 1].wait_recv()
        total += loc_r[d - 1].astype(F32)
    out_e[...] = total

    for k in range(2):
        out_r[2 * xl + k] = rx_s[xl, k]
    x_out.wait_recv()
    for k in range(2):
        out_r[2 * xp + k] = rx_r[k]

    pl.when(y >= 1)(up_out.wait_send)
    pl.when(y <= 1)(down_out.wait_send)
    pl.when(y >= 1)(low_out.wait_send)
    pl.when(y <= 1)(high_out.wait_send)
    pl.when(y == 2)(block_out[2].wait_send)
    pl.when(y == 1)(block_out[3].wait_send)
    pl.when(y <= 2)(on_up.wait_send)
    pl.when(y >= 1)(on_down.wait_send)
    for copy in (block_out[0], block_out[1], block_out[4], head_out, *term_out, pair_out, *y_out, *rep_out, *z_out, x_out):
        copy.wait_send()
    wait_all(asked.at[pl.ds(0, NBLK - 1)], a2a_sem.at[0])
    wait_all(served.at[pl.ds(0, (NBLK - 1) * 16)], a2a_sem.at[2])
    wait_all(back_s.at[pl.ds(0, (NBLK - 1) * 16)], a2a_sem.at[4])


def per_device(entity, relation, head_owner, head_row, query_rel, tail_row, neg_row):
    vmem = pl.BlockSpec(memory_space=pltpu.VMEM)
    dma = pltpu.SemaphoreType.DMA
    scratch = [
        pltpu.VMEM((D, D), BF16),
        pltpu.VMEM((4, D, D), BF16),
        pltpu.VMEM((1, 256), I32),
        pltpu.VMEM((1, 256), I32),
        pltpu.VMEM((4, 256), I32),
        pltpu.VMEM((4, 256), I32),
        pltpu.VMEM((1, 256), I32),
        pltpu.VMEM((128, 256), I32),
        pltpu.VMEM((256, 128), I32),
        pltpu.VMEM((NBLK, 1, 128), F32),
        pltpu.VMEM((NBLK, 1, 128), F32),
        pltpu.VMEM((NBLK, 128), F32),
        pltpu.VMEM((8, 1024), I32),
        pltpu.VMEM((1024, 256), BF16),
        pltpu.VMEM((1024, 256), BF16),
        pltpu.VMEM((STOPS * 256, D), BF16),
        pltpu.VMEM((2, 256, D), BF16),
        pltpu.VMEM((1024, D), BF16),
        pltpu.VMEM((256, D), BF16),
        pltpu.VMEM((D, 256), BF16),
        pltpu.VMEM((D, 256), BF16),
        pltpu.VMEM((4, 256, D), F32),
        pltpu.VMEM((1024, D), BF16),
        pltpu.VMEM((1024, 128), F32),
        pltpu.VMEM((1024, D), F32),
        pltpu.VMEM((1024, STOPS * 256), BF16),
        pltpu.VMEM((4, 256, D), BF16),
        pltpu.VMEM((2, 256, D), BF16),
        pltpu.VMEM((256, D), F32),
        pltpu.VMEM((STOPS - 1, 256, D), BF16),
        pltpu.VMEM((STOPS - 1, 256, D), BF16),
        pltpu.VMEM((2, 256, D), F32),
        pltpu.VMEM((2, 256, D), BF16),
        pltpu.VMEM((2, 256, D), F32),
        pltpu.VMEM((2, 256, D), BF16),
        pltpu.VMEM((2, 256, D), BF16),
        pltpu.VMEM((1024, 256), BF16),
        pltpu.VMEM((1024, 256), BF16),
        pltpu.VMEM((2, D, D), F32),
        pltpu.VMEM((2, D, D), BF16),
        pltpu.VMEM((NY - 1, 2, 128, D), BF16),
        pltpu.VMEM((2, 128, D), F32),
        pltpu.VMEM((2, 128, D), BF16),
        pltpu.VMEM((NZ - 1, 2, 16, D), BF16),
        pltpu.VMEM((NX, 2, 8, D), F32),
        pltpu.VMEM((2, 8, D), F32),
        pltpu.VMEM((4, D, 128), F32),
        pltpu.VMEM((4, D, 128), BF16),
        pltpu.VMEM((NREP - 1, D, 128), BF16),
        dma((7,)),
        dma((6,)),
        dma((10,)),
        dma((10,)),
        dma((4,)),
        dma((8,)),
        dma((6,)),
        dma((6,)),
        dma((14,)),
        dma((6,)),
    ]
    return pl.pallas_call(
        kernel,
        out_shape=(jax.ShapeDtypeStruct((D, 128), F32), jax.ShapeDtypeStruct((4, 8, D), F32)),
        in_specs=[pl.BlockSpec(memory_space=pl.ANY)] * 7,
        out_specs=(vmem, vmem),
        scratch_shapes=scratch,
        compiler_params=pltpu.CompilerParams(
            collective_id=0, has_side_effects=True, vmem_limit_bytes=61 * 2**20
        ),
        name="rescal_step",
    )(entity, relation, head_owner.T, head_row[None, :], query_rel.T, tail_row.T, neg_row)


def solution(mesh):
    placed = (
        P("blk", None),
        P("rep", None, None),
        P(("blk", "rep"), None),
        P(("blk", "rep")),
        P(("blk", "rep"), None),
        P(("blk", "rep"), None),
        P("blk", "rep"),
    )
    return jax.shard_map(
        per_device,
        mesh=mesh,
        in_specs=placed,
        out_specs=(P("blk", "rep"), P("rep", "blk", None)),
        check_vma=False,
    )
```

```python
import functools

import jax
import jax.numpy as jnp
from jax import lax
from jax.experimental import pallas as pl
from jax.experimental.pallas import tpu as pltpu
from jax.sharding import PartitionSpec as P

D = 512
STOPS = 6
NBLK, NY, NZ, NX, NREP = 64, 4, 8, 2, 4
OFFS = (0, 1, -1, 2, -2, 3)
MESH = pl.DeviceIdType.MESH
F32, BF16, I32 = jnp.float32, jnp.bfloat16, jnp.int32
NT = (((1,), (1,)), ((), ()))
TN = (((0,), (0,)), ((), ()))


def iota(shape, dim):
    return lax.broadcasted_iota(I32, shape, dim)


def hot(mask):
    return jnp.where(mask, 1.0, 0.0).astype(BF16)


def mm(a, b):
    return jnp.dot(a, b, preferred_element_type=F32)


def mm_nt(a, b):
    return lax.dot_general(a, b, NT, preferred_element_type=F32)


def mm_tn(a, b):
    return lax.dot_general(a, b, TN, preferred_element_type=F32)


def two_parts(value):
    high = value.astype(BF16)
    return high, (value - high.astype(F32)).astype(BF16)


def kernel(
    ent_h, rel_h, owner_h, row_h, kind_h, tail_h, neg_h, out_e, out_r,
    ent, rel, owner_v, row_v, kind_v, tail_v, neg_v, rows, cols, asked, wanted, wanted2, w_row, served, fetched, blocks, relay, tails, head, head_t, head_p,
    prod, query, pos_w, grad_q, weights, pair, pair_p, term_own, term_s, term_r, term_f, relay_s, relay_r, back_s, back_r,
    rel_f, rel_s, rel_y, rz_f, rz_s, rz_r, rx_s, rx_r, loc, loc_s, loc_r,
    in_sem, a2a_sem, nb_sem, gt_sem, hop_sem, x_sem, y_sem, z_sem, rep_sem,
):
    b, r = lax.axis_index("blk"), lax.axis_index("rep")
    y, z, xl = lax.rem(b, NY), lax.rem(lax.div(b, NY), NZ), lax.div(b, NY * NZ)
    xp = 1 - xl
    other_x = lax.rem(b + NY * NZ, NBLK)

    def remote(src, dst, s_sem, r_sem, blk, rep):
        return pltpu.make_async_remote_copy(
            src_ref=src, dst_ref=dst, send_sem=s_sem, recv_sem=r_sem, device_id=(blk, rep), device_id_type=MESH
        )

    def send(*copy_args):
        copy = remote(*copy_args)
        copy.start()
        return copy

    def block(n):
        return blocks.at[pl.ds(n * 256, 256)]

    def wait_all(ref, sem):
        pltpu.make_async_copy(ref, ref, sem).wait()

    def to_all(src, dst, s_sem, r_sem):
        def step(k, carry):
            peer = lax.rem(b + k, NBLK)
            send(src(peer), dst, s_sem, r_sem, peer, r)
            return carry

        lax.fori_loop(1, NBLK, step, 0)

    def rows16(ref):
        return lambda s: ref.at[pl.ds(pl.multiple_of(s * 16, 16), 16)]

    barrier = pltpu.get_barrier_semaphore()

    def greet(k, carry):
        pl.semaphore_signal(barrier, inc=1, device_id=(lax.rem(b + k, NBLK), r), device_id_type=MESH)
        return carry

    lax.fori_loop(1, NBLK, greet, 0)
    for d in range(1, NREP):
        pl.semaphore_signal(barrier, inc=1, device_id=(b, lax.rem(r + d, NREP)), device_id_type=MESH)

    index_in = []
    for n, (src, dst) in enumerate(
        ((owner_h, owner_v), (row_h, row_v), (kind_h, kind_v), (tail_h, tail_v), (neg_h, neg_v))
    ):
        index_in.append(pltpu.make_async_copy(src, dst, in_sem.at[n]))
    ent_in = pltpu.make_async_copy(ent_h, ent, in_sem.at[5])
    rel_in = pltpu.make_async_copy(rel_h, rel, in_sem.at[6])
    for copy in (*index_in, ent_in, rel_in):
        copy.start()
    for copy in index_in:
        copy.wait()
    rows[...] = jnp.zeros_like(rows)
    rows[0:1, :] = owner_v[...]
    rows[1:2, :] = row_v[...]
    rows[2:6, :] = kind_v[...]
    rows[6:10, :] = tail_v[...]
    rows[10:11, :] = neg_v[...]
    cols[...] = jnp.transpose(rows[...])

    owner_row, owner_col = rows[0:1, :], cols[:, 0:1]
    in_shard = iota((NBLK, 256), 0) == owner_row
    shard_hot = hot(in_shard)
    before = mm(shard_hot, hot(iota((256, 256), 0) < iota((256, 256), 1)))
    slot_row = jnp.sum(jnp.where(in_shard, before, 0.0), axis=0, keepdims=True)
    place_row = owner_row * 16 + slot_row.astype(I32)
    of_head = iota((256, 128), 1) == owner_col
    before = mm(hot(iota((256, 256), 1) < iota((256, 256), 0)), hot(of_head))
    slot_col = jnp.sum(jnp.where(of_head, before, 0.0), axis=1, keepdims=True).astype(I32)
    place_col = owner_col * 16 + slot_col
    named = cols[:, 1:2] + 1
    lane = iota((256, 128), 1)
    digits = jnp.where(lane == slot_col, named >> 5, 0) + jnp.where(lane == slot_col + 64, named & 31, 0)
    requests = mm(shard_hot, digits.astype(F32).astype(BF16))
    for s in range(NBLK):
        asked[s] = requests[s : s + 1, :]
    ent_in.wait()
    block(0)[...] = mm(hot(iota((256, D), 1) == cols[:, 10:11]), ent[...]).astype(BF16)
    rel_in.wait()

    pl.semaphore_wait(barrier, NBLK - 1 + NREP - 1)
    to_all(lambda s: asked.at[s], wanted.at[b], a2a_sem.at[0], a2a_sem.at[1])
    wanted[b] = asked[b]

    plane_up, plane_down = lax.rem(b + NY, NBLK), lax.rem(b + NBLK - NY, NBLK)
    up_out = remote(block(0), relay.at[0], hop_sem.at[0], hop_sem.at[1], plane_up, r)
    down_out = remote(block(0), relay.at[1], hop_sem.at[2], hop_sem.at[3], plane_down, r)
    pl.when(y >= 1)(up_out.start)
    pl.when(y <= 1)(down_out.start)
    block_out, block_far = [], []
    for n in range(1, STOPS):
        visitor = b - y + lax.rem(y + OFFS[n] + NY, NY)
        sems = nb_sem.at[n - 1], nb_sem.at[4 + n]
        block_out.append(remote(block(0), block(n), *sems, visitor, r))
        block_far.append(remote(relay.at[0 if OFFS[n] > 0 else 1], block(n), *sems, visitor, r))
        pl.when((y + OFFS[n] >= 0) & (y + OFFS[n] < NY))(block_out[n - 1].start)
    for j in range(2):
        tails[j * 256 : (j + 1) * 256] = mm(hot(iota((256, D), 1) == cols[:, 6 + j : 7 + j]), ent[...]).astype(BF16)
    wait_all(wanted.at[pl.ds(0, NBLK - 1)], a2a_sem.at[1])

    for s in range(NBLK):
        wanted2[s : s + 1, :] = wanted[s]
    spread = mm(hot(iota((1024, NBLK), 0) >> 4 == iota((1024, NBLK), 1)), wanted2[...].astype(BF16))
    k_of, lane = iota((1024, 128), 0) & 7, iota((1024, 128), 1)
    spread = jnp.where(lane == k_of, spread * 32.0, jnp.where(lane == k_of + 64, spread, 0.0))
    w_row[...] = mm_nt(jnp.ones((8, 128), BF16), spread.astype(BF16)).astype(I32) - 1
    w_col = jnp.sum(spread, axis=1, keepdims=True).astype(I32) - 1
    first_half = (iota((256, 256), 0) >> 3 & 1) == 0
    for t in range(4):
        whole = mm(hot(iota((256, D), 1) == w_col[t * 256 : (t + 1) * 256]), ent[...])
        served[t * 256 : (t + 1) * 256] = jnp.where(first_half, whole[:, :256], whole[:, 256:]).astype(BF16)
    mine = pl.ds(pl.multiple_of(b * 16, 16), 16)
    to_all(rows16(served), fetched.at[mine], a2a_sem.at[2], a2a_sem.at[3])
    fetched[mine] = served[mine]
    pl.when(y >= 1)(up_out.wait_recv)
    pl.when(y <= 1)(down_out.wait_recv)
    for n in range(1, STOPS):
        pl.when((y + OFFS[n] < 0) | (y + OFFS[n] >= NY))(block_far[n - 1].start)
    for j in range(2, 4):
        tails[j * 256 : (j + 1) * 256] = mm(hot(iota((256, D), 1) == cols[:, 6 + j : 7 + j]), ent[...]).astype(BF16)
    wait_all(fetched.at[pl.ds(0, (NBLK - 1) * 16)], a2a_sem.at[3])
    for h in range(2):
        picked = hot(iota((256, 1024), 1) == place_col + 8 * h)
        head[:, h * 256 : (h + 1) * 256] = mm(picked, fetched[...]).astype(BF16)

    for k in range(4):
        prod[k] = mm(head[...], rel[k])

    def query_rows(t, carry):
        at = pl.ds(pl.multiple_of(t * 16, 16), 16)
        kind = cols[at, :]
        for j in range(4):
            to = pl.ds(pl.multiple_of(j * 256 + t * 16, 16), 16)
            q = prod[0, at, :]
            for k in range(1, 4):
                q = jnp.where(kind[:, 2 + j : 3 + j] == k, prod[k, at, :], q)
            q = q.astype(BF16)
            query[to, :] = q
        return carry

    lax.fori_loop(0, 16, query_rows, 0, unroll=2)

    def positive_rows(t, carry):
        at = pl.ds(pl.multiple_of(t * 32, 32), 32)
        tail = tails[at, :].astype(F32)
        score = jnp.sum(query[at, :].astype(F32) * tail, axis=1, keepdims=True)
        weight = jax.nn.sigmoid(score) - 1.0
        grad_q[at, :] = weight * tail
        pos_w[at, :] = jnp.broadcast_to(weight, (32, 128))
        return carry

    term_out = []

    def visit(n):
        met = slice(n * 256, (n + 1) * 256)
        weights[:, met] = (jax.nn.sigmoid(mm_nt(query[...], block(n)[...])) * (1.0 / STOPS)).astype(BF16)
        return mm_tn(weights[:, met], query[...])

    for n in range(1, STOPS):
        if n == 3:
            c = iota((D, D), 0)
            natural = (c >> 3 & 1) * 256 + (c >> 4 & 7) * 32 + (c >> 7) * 8 + (c & 7)
            head_t[...] = mm_nt(hot(iota((D, D), 1) == natural), head[...]).astype(BF16)
            head_out = send(head_t, head_p, x_sem.at[0], x_sem.at[1], other_x, r)
            lax.fori_loop(0, 32, positive_rows, 0, unroll=4)
            term_own[...] = visit(0)
        block_out[n - 1].wait_recv()
        term_s[n - 1] = visit(n).astype(BF16)
        via = b - y + lax.rem(y - OFFS[n] + NY, NY)
        term_out.append(send(term_s.at[n - 1], term_r.at[n - 1], gt_sem.at[n - 1], gt_sem.at[4 + n], via, r))
    for j in range(4):
        at = slice(j * 256, (j + 1) * 256)
        grad_q[at, :] += mm(weights[at, :], blocks[...])

    def pair_rows(t, carry):
        at = pl.ds(pl.multiple_of(t * 16, 16), 16)
        kind = cols[at, :]
        for k in range(4):
            total = jnp.zeros((16, D), F32)
            for j in range(4):
                total += jnp.where(kind[:, 2 + j : 3 + j] == k, grad_q[pl.ds(pl.multiple_of(j * 256 + t * 16, 16), 16), :], 0.0)
            pair[k, at, :] = total.astype(BF16)
        return carry

    lax.fori_loop(0, 16, pair_rows, 0, unroll=2)
    pair_out = send(pair.at[pl.ds(2 * xp, 2)], pair_p, x_sem.at[2], x_sem.at[3], other_x, r)

    grad_head = mm_nt(pair[0], rel[0])
    for k in range(1, 4):
        grad_head += mm_nt(pair[k], rel[k])
    grad_head = grad_head.astype(BF16)
    for t in range(4):
        q = iota((256, 256), 0) + t * 256
        whole = mm(hot(q - (q >> 3 & 1) * 8 == place_row), grad_head)
        back_s[t * 256 : (t + 1) * 256] = jnp.where(first_half, whole[:, :256], whole[:, 256:]).astype(BF16)
    to_all(rows16(back_s), back_r.at[mine], a2a_sem.at[4], a2a_sem.at[5])
    back_r[mine] = back_s[mine]

    head_out.wait_recv()
    pair_out.wait_recv()
    for k in range(2):
        rel_f[k] = mm(head_t[...], pair[2 * xl + k]) + mm(head_p[...], pair_p[k])
        rel_s[k] = rel_f[k].astype(BF16)
    y_out = []
    for d in range(1, NY):
        yp = lax.rem(y + d, NY)
        part = rel_s.at[:, pl.ds(pl.multiple_of(yp * 128, 128), 128), :]
        y_out.append(send(part, rel_y.at[d - 1], y_sem.at[d - 1], y_sem.at[2 + d], b - y + yp, r))

    for j in range(4):
        onto = hot(iota((D, 256), 0) == rows[6 + j : 7 + j, :])
        high, low = two_parts(pos_w[j * 256 : (j + 1) * 256, 0:1] * query[j * 256 : (j + 1) * 256, :].astype(F32))
        part = mm(onto, high) + mm(onto, low)
        for c in range(4):
            loc[c] = part[:, c * 128 : (c + 1) * 128] if j == 0 else loc[c] + part[:, c * 128 : (c + 1) * 128]

    term_f[...] = jnp.zeros_like(term_f)
    for n in range(1, STOPS):
        term_out[n - 1].wait_recv()

        def own(n=n):
            term_own[...] += term_r[n - 1].astype(F32)

        def other(n=n):
            term_f[0 if OFFS[n] > 0 else 1] += term_r[n - 1].astype(F32)

        pl.when((y + OFFS[n] >= 0) & (y + OFFS[n] < NY))(own)
        pl.when((y + OFFS[n] < 0) | (y + OFFS[n] >= NY))(other)
    relay_s[...] = term_f[...].astype(BF16)
    low_out = remote(relay_s.at[0], relay_r.at[0], hop_sem.at[4], hop_sem.at[5], plane_down, r)
    high_out = remote(relay_s.at[1], relay_r.at[1], hop_sem.at[6], hop_sem.at[7], plane_up, r)
    pl.when(y >= 1)(low_out.start)
    pl.when(y <= 1)(high_out.start)

    wait_all(back_r.at[pl.ds(0, (NBLK - 1) * 16)], a2a_sem.at[5])
    lanes = iota((D, 1024), 1)
    for h in range(2):
        onto = hot((iota((D, 1024), 0) == w_row[0:1, :]) & ((lanes >> 3 & 1) == h))
        part = mm(onto, back_r[...])
        for c in range(2):
            loc[2 * h + c] += part[:, c * 128 : (c + 1) * 128]

    rz_f[...] = rel_f[:, pl.ds(pl.multiple_of(y * 128, 128), 128), :]
    for d in range(1, NY):
        y_out[d - 1].wait_recv()
        rz_f[...] += rel_y[d - 1].astype(F32)
    rz_s[...] = rz_f[...].astype(BF16)
    z_out = []
    for d in range(1, NZ):
        zp = lax.rem(z + d, NZ)
        part = rz_s.at[:, pl.ds(pl.multiple_of(zp * 16, 16), 16), :]
        z_out.append(send(part, rz_r.at[d - 1], z_sem.at[d - 1], z_sem.at[6 + d], b + (zp - z) * NY, r))

    def from_above():
        low_out.wait_recv()
        term_own[...] += relay_r[0].astype(F32)

    def from_below():
        high_out.wait_recv()
        term_own[...] += relay_r[1].astype(F32)

    pl.when(y >= 1)(from_above)
    pl.when(y <= 1)(from_below)
    onto = hot(iota((D, 256), 0) == rows[10:11, :])
    high, low = two_parts(term_own[...])
    part = mm(onto, high) + mm(onto, low)
    for c in range(4):
        loc[c] += part[:, c * 128 : (c + 1) * 128]
        loc_s[c] = loc[c].astype(BF16)
    rep_out = []
    for d in range(1, NREP):
        rp = lax.rem(r + d, NREP)
        rep_out.append(send(loc_s.at[rp], loc_r.at[d - 1], rep_sem.at[d - 1], rep_sem.at[2 + d], b, rp))

    total = rz_f[:, pl.ds(pl.multiple_of(z * 16, 16), 16), :]
    for d in range(1, NZ):
        z_out[d - 1].wait_recv()
        total += rz_r[d - 1].astype(F32)
    for x in range(NX):
        rx_s[x] = total[:, x * 8 : (x + 1) * 8, :]
    x_out = send(rx_s.at[xp], rx_r, x_sem.at[4], x_sem.at[5], other_x, r)
    total = loc[r]
    for d in range(1, NREP):
        rep_out[d - 1].wait_recv()
        total += loc_r[d - 1].astype(F32)
    out_e[...] = total

    for k in range(2):
        out_r[2 * xl + k] = rx_s[xl, k]
    x_out.wait_recv()
    for k in range(2):
        out_r[2 * xp + k] = rx_r[k]

    pl.when(y >= 1)(up_out.wait_send)
    pl.when(y <= 1)(down_out.wait_send)
    pl.when(y >= 1)(low_out.wait_send)
    pl.when(y <= 1)(high_out.wait_send)
    for copy in (*block_out, head_out, *term_out, pair_out, *y_out, *rep_out, *z_out, x_out):
        copy.wait_send()
    wait_all(asked.at[pl.ds(0, NBLK - 1)], a2a_sem.at[0])
    wait_all(served.at[pl.ds(0, (NBLK - 1) * 16)], a2a_sem.at[2])
    wait_all(back_s.at[pl.ds(0, (NBLK - 1) * 16)], a2a_sem.at[4])


def per_device(entity, relation, head_owner, head_row, query_rel, tail_row, neg_row):
    vmem = pl.BlockSpec(memory_space=pltpu.VMEM)
    dma = pltpu.SemaphoreType.DMA
    scratch = [
        pltpu.VMEM((D, D), BF16),
        pltpu.VMEM((4, D, D), BF16),
        pltpu.VMEM((1, 256), I32),
        pltpu.VMEM((1, 256), I32),
        pltpu.VMEM((4, 256), I32),
        pltpu.VMEM((4, 256), I32),
        pltpu.VMEM((1, 256), I32),
        pltpu.VMEM((128, 256), I32),
        pltpu.VMEM((256, 128), I32),
        pltpu.VMEM((NBLK, 1, 128), F32),
        pltpu.VMEM((NBLK, 1, 128), F32),
        pltpu.VMEM((NBLK, 128), F32),
        pltpu.VMEM((8, 1024), I32),
        pltpu.VMEM((1024, 256), BF16),
        pltpu.VMEM((1024, 256), BF16),
        pltpu.VMEM((STOPS * 256, D), BF16),
        pltpu.VMEM((2, 256, D), BF16),
        pltpu.VMEM((1024, D), BF16),
        pltpu.VMEM((256, D), BF16),
        pltpu.VMEM((D, 256), BF16),
        pltpu.VMEM((D, 256), BF16),
        pltpu.VMEM((4, 256, D), F32),
        pltpu.VMEM((1024, D), BF16),
        pltpu.VMEM((1024, 128), F32),
        pltpu.VMEM((1024, D), F32),
        pltpu.VMEM((1024, STOPS * 256), BF16),
        pltpu.VMEM((4, 256, D), BF16),
        pltpu.VMEM((2, 256, D), BF16),
        pltpu.VMEM((256, D), F32),
        pltpu.VMEM((STOPS - 1, 256, D), BF16),
        pltpu.VMEM((STOPS - 1, 256, D), BF16),
        pltpu.VMEM((2, 256, D), F32),
        pltpu.VMEM((2, 256, D), BF16),
        pltpu.VMEM((2, 256, D), BF16),
        pltpu.VMEM((1024, 256), BF16),
        pltpu.VMEM((1024, 256), BF16),
        pltpu.VMEM((2, D, D), F32),
        pltpu.VMEM((2, D, D), BF16),
        pltpu.VMEM((NY - 1, 2, 128, D), BF16),
        pltpu.VMEM((2, 128, D), F32),
        pltpu.VMEM((2, 128, D), BF16),
        pltpu.VMEM((NZ - 1, 2, 16, D), BF16),
        pltpu.VMEM((NX, 2, 8, D), F32),
        pltpu.VMEM((2, 8, D), F32),
        pltpu.VMEM((4, D, 128), F32),
        pltpu.VMEM((4, D, 128), BF16),
        pltpu.VMEM((NREP - 1, D, 128), BF16),
        dma((7,)),
        dma((6,)),
        dma((10,)),
        dma((10,)),
        dma((8,)),
        dma((6,)),
        dma((6,)),
        dma((14,)),
        dma((6,)),
    ]
    return pl.pallas_call(
        kernel,
        out_shape=(jax.ShapeDtypeStruct((D, 128), F32), jax.ShapeDtypeStruct((4, 8, D), F32)),
        in_specs=[pl.BlockSpec(memory_space=pl.ANY)] * 7,
        out_specs=(vmem, vmem),
        scratch_shapes=scratch,
        compiler_params=pltpu.CompilerParams(
            collective_id=0, has_side_effects=True, vmem_limit_bytes=61 * 2**20
        ),
        name="rescal_step",
    )(entity, relation, head_owner.T, head_row[None, :], query_rel.T, tail_row.T, neg_row)


def solution(mesh):
    placed = (
        P("blk", None),
        P("rep", None, None),
        P(("blk", "rep"), None),
        P(("blk", "rep")),
        P(("blk", "rep"), None),
        P(("blk", "rep"), None),
        P("blk", "rep"),
    )
    return jax.shard_map(
        per_device,
        mesh=mesh,
        in_specs=placed,
        out_specs=(P("blk", "rep"), P("rep", "blk", None)),
        check_vma=False,
    )
```

```python
import functools

import jax
import jax.numpy as jnp
from jax import lax
from jax.experimental import pallas as pl
from jax.experimental.pallas import tpu as pltpu
from jax.sharding import PartitionSpec as P

D = 512
STOPS = 6
NBLK, NY, NZ, NX, NREP = 64, 4, 8, 2, 4
OFFS = (0, 1, -1, 2, -2, 3)
MESH = pl.DeviceIdType.MESH
F32, BF16, I32 = jnp.float32, jnp.bfloat16, jnp.int32
NT = (((1,), (1,)), ((), ()))
TN = (((0,), (0,)), ((), ()))


def iota(shape, dim):
    return lax.broadcasted_iota(I32, shape, dim)


def hot(mask):
    return jnp.where(mask, 1.0, 0.0).astype(BF16)


def mm(a, b):
    return jnp.dot(a, b, preferred_element_type=F32)


def mm_nt(a, b):
    return lax.dot_general(a, b, NT, preferred_element_type=F32)


def mm_tn(a, b):
    return lax.dot_general(a, b, TN, preferred_element_type=F32)


def two_parts(value):
    high = value.astype(BF16)
    return high, (value - high.astype(F32)).astype(BF16)


def kernel(
    ent_h, rel_h, owner_h, row_h, kind_h, tail_h, neg_h, out_e, out_r,
    ent, rel, owner_v, row_v, kind_v, tail_v, neg_v, rows, cols, asked, wanted, wanted2, w_row, served, fetched, blocks, relay, tails, head, head_t, head_p,
    prod, query, pos_w, grad_q, weights, pair, pair_p, term_own, term_s, term_r, term_f, relay_s, relay_r, back_s, back_r,
    rel_f, rel_s, rel_y, rz_f, rz_s, rz_r, rx_s, rx_r, loc, loc_s, loc_r,
    in_sem, a2a_sem, nb_sem, chain_sem, gt_sem, hop_sem, x_sem, y_sem, z_sem, rep_sem,
):
    b, r = lax.axis_index("blk"), lax.axis_index("rep")
    y, z, xl = lax.rem(b, NY), lax.rem(lax.div(b, NY), NZ), lax.div(b, NY * NZ)
    xp = 1 - xl
    other_x = lax.rem(b + NY * NZ, NBLK)

    def remote(src, dst, s_sem, r_sem, blk, rep):
        return pltpu.make_async_remote_copy(
            src_ref=src, dst_ref=dst, send_sem=s_sem, recv_sem=r_sem, device_id=(blk, rep), device_id_type=MESH
        )

    def send(*copy_args):
        copy = remote(*copy_args)
        copy.start()
        return copy

    def block(n):
        return blocks.at[pl.ds(n * 256, 256)]

    def wait_all(ref, sem):
        pltpu.make_async_copy(ref, ref, sem).wait()

    def to_all(src, dst, s_sem, r_sem):
        def step(k, carry):
            peer = lax.rem(b + k, NBLK)
            send(src(peer), dst, s_sem, r_sem, peer, r)
            return carry

        lax.fori_loop(1, NBLK, step, 0)

    def rows16(ref):
        return lambda s: ref.at[pl.ds(pl.multiple_of(s * 16, 16), 16)]

    barrier = pltpu.get_barrier_semaphore()

    def greet(k, carry):
        pl.semaphore_signal(barrier, inc=1, device_id=(lax.rem(b + k, NBLK), r), device_id_type=MESH)
        return carry

    lax.fori_loop(1, NBLK, greet, 0)
    for d in range(1, NREP):
        pl.semaphore_signal(barrier, inc=1, device_id=(b, lax.rem(r + d, NREP)), device_id_type=MESH)

    index_in = []
    for n, (src, dst) in enumerate(
        ((owner_h, owner_v), (row_h, row_v), (kind_h, kind_v), (tail_h, tail_v), (neg_h, neg_v))
    ):
        index_in.append(pltpu.make_async_copy(src, dst, in_sem.at[n]))
    ent_in = pltpu.make_async_copy(ent_h, ent, in_sem.at[5])
    rel_in = pltpu.make_async_copy(rel_h, rel, in_sem.at[6])
    for copy in (*index_in, ent_in, rel_in):
        copy.start()
    for copy in index_in:
        copy.wait()
    rows[...] = jnp.zeros_like(rows)
    rows[0:1, :] = owner_v[...]
    rows[1:2, :] = row_v[...]
    rows[2:6, :] = kind_v[...]
    rows[6:10, :] = tail_v[...]
    rows[10:11, :] = neg_v[...]
    cols[...] = jnp.transpose(rows[...])

    owner_row, owner_col = rows[0:1, :], cols[:, 0:1]
    in_shard = iota((NBLK, 256), 0) == owner_row
    shard_hot = hot(in_shard)
    before = mm(shard_hot, hot(iota((256, 256), 0) < iota((256, 256), 1)))
    slot_row = jnp.sum(jnp.where(in_shard, before, 0.0), axis=0, keepdims=True)
    place_row = owner_row * 16 + slot_row.astype(I32)
    of_head = iota((256, 128), 1) == owner_col
    before = mm(hot(iota((256, 256), 1) < iota((256, 256), 0)), hot(of_head))
    slot_col = jnp.sum(jnp.where(of_head, before, 0.0), axis=1, keepdims=True).astype(I32)
    place_col = owner_col * 16 + slot_col
    named = cols[:, 1:2] + 1
    lane = iota((256, 128), 1)
    digits = jnp.where(lane == slot_col, named >> 5, 0) + jnp.where(lane == slot_col + 64, named & 31, 0)
    requests = mm(shard_hot, digits.astype(F32).astype(BF16))
    for s in range(NBLK):
        asked[s] = requests[s : s + 1, :]
    ent_in.wait()
    block(0)[...] = mm(hot(iota((256, D), 1) == cols[:, 10:11]), ent[...]).astype(BF16)
    rel_in.wait()

    pl.semaphore_wait(barrier, NBLK - 1 + NREP - 1)
    to_all(lambda s: asked.at[s], wanted.at[b], a2a_sem.at[0], a2a_sem.at[1])
    wanted[b] = asked[b]

    plane_up, plane_down = lax.rem(b + NY, NBLK), lax.rem(b + NBLK - NY, NBLK)
    up_out = remote(block(0), relay.at[0], hop_sem.at[0], hop_sem.at[1], plane_up, r)
    down_out = remote(block(0), relay.at[1], hop_sem.at[2], hop_sem.at[3], plane_down, r)
    pl.when(y >= 1)(up_out.start)
    pl.when(y <= 1)(down_out.start)
    block_out, block_far = [], []
    for n in range(1, STOPS):
        visitor = b - y + lax.rem(y + OFFS[n] + NY, NY)
        sems = nb_sem.at[n - 1], nb_sem.at[4 + n]
        block_out.append(remote(block(0), block(n), *sems, visitor, r))
        block_far.append(remote(relay.at[0 if OFFS[n] > 0 else 1], block(n), *sems, visitor, r))
        if abs(OFFS[n]) != 2:
            pl.when((y + OFFS[n] >= 0) & (y + OFFS[n] < NY))(block_out[n - 1].start)
    for j in range(2):
        tails[j * 256 : (j + 1) * 256] = mm(hot(iota((256, D), 1) == cols[:, 6 + j : 7 + j]), ent[...]).astype(BF16)
    wait_all(wanted.at[pl.ds(0, NBLK - 1)], a2a_sem.at[1])

    for s in range(NBLK):
        wanted2[s : s + 1, :] = wanted[s]
    spread = mm(hot(iota((1024, NBLK), 0) >> 4 == iota((1024, NBLK), 1)), wanted2[...].astype(BF16))
    k_of, lane = iota((1024, 128), 0) & 7, iota((1024, 128), 1)
    spread = jnp.where(lane == k_of, spread * 32.0, jnp.where(lane == k_of + 64, spread, 0.0))
    w_row[...] = mm_nt(jnp.ones((8, 128), BF16), spread.astype(BF16)).astype(I32) - 1
    w_col = jnp.sum(spread, axis=1, keepdims=True).astype(I32) - 1
    first_half = (iota((256, 256), 0) >> 3 & 1) == 0
    for t in range(4):
        whole = mm(hot(iota((256, D), 1) == w_col[t * 256 : (t + 1) * 256]), ent[...])
        served[t * 256 : (t + 1) * 256] = jnp.where(first_half, whole[:, :256], whole[:, 256:]).astype(BF16)
    mine = pl.ds(pl.multiple_of(b * 16, 16), 16)
    to_all(rows16(served), fetched.at[mine], a2a_sem.at[2], a2a_sem.at[3])
    fetched[mine] = served[mine]
    pl.when(y >= 1)(up_out.wait_recv)
    pl.when(y <= 1)(down_out.wait_recv)
    for n in (1, 2, 5):
        pl.when((y + OFFS[n] < 0) | (y + OFFS[n] >= NY))(block_far[n - 1].start)
    pl.when(y == 2)(block_far[2].start)
    pl.when(y == 1)(block_far[3].start)
    next_y, last_y = b - y + lax.rem(y + 1, NY), b - y + lax.rem(y + NY - 1, NY)
    on_up = remote(block(1), block(3), chain_sem.at[0], nb_sem.at[7], next_y, r)
    on_down = remote(block(2), block(4), chain_sem.at[1], nb_sem.at[8], last_y, r)

    def pass_up():
        block_out[0].wait_recv()
        on_up.start()

    def pass_down():
        block_out[1].wait_recv()
        on_down.start()

    pl.when((y >= 1) & (y <= 2))(pass_up)
    pl.when((y >= 1) & (y <= 2))(pass_down)
    for j in range(2, 4):
        tails[j * 256 : (j + 1) * 256] = mm(hot(iota((256, D), 1) == cols[:, 6 + j : 7 + j]), ent[...]).astype(BF16)
    wait_all(fetched.at[pl.ds(0, (NBLK - 1) * 16)], a2a_sem.at[3])
    for h in range(2):
        picked = hot(iota((256, 1024), 1) == place_col + 8 * h)
        head[:, h * 256 : (h + 1) * 256] = mm(picked, fetched[...]).astype(BF16)

    for k in range(4):
        prod[k] = mm(head[...], rel[k])

    def query_rows(t, carry):
        at = pl.ds(pl.multiple_of(t * 16, 16), 16)
        kind = cols[at, :]
        for j in range(4):
            to = pl.ds(pl.multiple_of(j * 256 + t * 16, 16), 16)
            q = prod[0, at, :]
            for k in range(1, 4):
                q = jnp.where(kind[:, 2 + j : 3 + j] == k, prod[k, at, :], q)
            q = q.astype(BF16)
            query[to, :] = q
            tail = tails[to, :].astype(F32)
            score = jnp.sum(q.astype(F32) * tail, axis=1, keepdims=True)
            weight = jax.nn.sigmoid(score) - 1.0
            grad_q[to, :] = weight * tail
            pos_w[to, :] = jnp.broadcast_to(weight, (16, 128))
        return carry

    lax.fori_loop(0, 16, query_rows, 0, unroll=2)

    pl.when(y == 0)(pass_up)
    pl.when(y == 3)(pass_down)
    pl.when(y == 3)(block_out[0].wait_recv)
    pl.when(y == 0)(block_out[1].wait_recv)

    c = iota((D, D), 0)
    natural = (c >> 3 & 1) * 256 + (c >> 4 & 7) * 32 + (c >> 7) * 8 + (c & 7)
    head_t[...] = mm_nt(hot(iota((D, D), 1) == natural), head[...]).astype(BF16)
    head_out = send(head_t, head_p, x_sem.at[0], x_sem.at[1], other_x, r)

    term_out = []
    for n in range(STOPS):
        if n > 2:
            block_out[n - 1].wait_recv()
        met = slice(n * 256, (n + 1) * 256)
        weights[:, met] = (jax.nn.sigmoid(mm_nt(query[...], block(n)[...])) * (1.0 / STOPS)).astype(BF16)
        term = mm_tn(weights[:, met], query[...])
        if n == 0:
            term_own[...] = term
        else:
            term_s[n - 1] = term.astype(BF16)
            via = b - y + lax.rem(y - OFFS[n] + NY, NY)
            term_out.append(send(term_s.at[n - 1], term_r.at[n - 1], gt_sem.at[n - 1], gt_sem.at[4 + n], via, r))
        for upto, since in ((4, 0), (STOPS, 4)):
            if n == upto - 1:
                met = slice(since * 256, upto * 256)
                for j in range(4):
                    at = slice(j * 256, (j + 1) * 256)
                    grad_q[at, :] += mm(weights[at, met], blocks[met, :])

    def pair_rows(t, carry):
        at = pl.ds(pl.multiple_of(t * 16, 16), 16)
        kind = cols[at, :]
        for k in range(4):
            total = jnp.zeros((16, D), F32)
            for j in range(4):
                total += jnp.where(kind[:, 2 + j : 3 + j] == k, grad_q[pl.ds(pl.multiple_of(j * 256 + t * 16, 16), 16), :], 0.0)
            pair[k, at, :] = total.astype(BF16)
        return carry

    lax.fori_loop(0, 16, pair_rows, 0, unroll=2)
    pair_out = send(pair.at[pl.ds(2 * xp, 2)], pair_p, x_sem.at[2], x_sem.at[3], other_x, r)

    grad_head = mm_nt(pair[0], rel[0])
    for k in range(1, 4):
        grad_head += mm_nt(pair[k], rel[k])
    grad_head = grad_head.astype(BF16)
    for t in range(4):
        q = iota((256, 256), 0) + t * 256
        whole = mm(hot(q - (q >> 3 & 1) * 8 == place_row), grad_head)
        back_s[t * 256 : (t + 1) * 256] = jnp.where(first_half, whole[:, :256], whole[:, 256:]).astype(BF16)
    to_all(rows16(back_s), back_r.at[mine], a2a_sem.at[4], a2a_sem.at[5])
    back_r[mine] = back_s[mine]

    head_out.wait_recv()
    pair_out.wait_recv()
    for k in range(2):
        rel_f[k] = mm(head_t[...], pair[2 * xl + k]) + mm(head_p[...], pair_p[k])
        rel_s[k] = rel_f[k].astype(BF16)
    y_out = []
    for d in range(1, NY):
        yp = lax.rem(y + d, NY)
        part = rel_s.at[:, pl.ds(pl.multiple_of(yp * 128, 128), 128), :]
        y_out.append(send(part, rel_y.at[d - 1], y_sem.at[d - 1], y_sem.at[2 + d], b - y + yp, r))

    for j in range(4):
        onto = hot(iota((D, 256), 0) == rows[6 + j : 7 + j, :])
        high, low = two_parts(pos_w[j * 256 : (j + 1) * 256, 0:1] * query[j * 256 : (j + 1) * 256, :].astype(F32))
        part = mm(onto, high) + mm(onto, low)
        for c in range(4):
            loc[c] = part[:, c * 128 : (c + 1) * 128] if j == 0 else loc[c] + part[:, c * 128 : (c + 1) * 128]

    term_f[...] = jnp.zeros_like(term_f)
    for n in range(1, STOPS):
        term_out[n - 1].wait_recv()

        def own(n=n):
            term_own[...] += term_r[n - 1].astype(F32)

        def other(n=n):
            term_f[0 if OFFS[n] > 0 else 1] += term_r[n - 1].astype(F32)

        pl.when((y + OFFS[n] >= 0) & (y + OFFS[n] < NY))(own)
        pl.when((y + OFFS[n] < 0) | (y + OFFS[n] >= NY))(other)
    relay_s[...] = term_f[...].astype(BF16)
    low_out = remote(relay_s.at[0], relay_r.at[0], hop_sem.at[4], hop_sem.at[5], plane_down, r)
    high_out = remote(relay_s.at[1], relay_r.at[1], hop_sem.at[6], hop_sem.at[7], plane_up, r)
    pl.when(y >= 1)(low_out.start)
    pl.when(y <= 1)(high_out.start)

    wait_all(back_r.at[pl.ds(0, (NBLK - 1) * 16)], a2a_sem.at[5])
    lanes = iota((D, 1024), 1)
    for h in range(2):
        onto = hot((iota((D, 1024), 0) == w_row[0:1, :]) & ((lanes >> 3 & 1) == h))
        part = mm(onto, back_r[...])
        for c in range(2):
            loc[2 * h + c] += part[:, c * 128 : (c + 1) * 128]

    rz_f[...] = rel_f[:, pl.ds(pl.multiple_of(y * 128, 128), 128), :]
    for d in range(1, NY):
        y_out[d - 1].wait_recv()
        rz_f[...] += rel_y[d - 1].astype(F32)
    rz_s[...] = rz_f[...].astype(BF16)
    z_out = []
    for d in range(1, NZ):
        zp = lax.rem(z + d, NZ)
        part = rz_s.at[:, pl.ds(pl.multiple_of(zp * 16, 16), 16), :]
        z_out.append(send(part, rz_r.at[d - 1], z_sem.at[d - 1], z_sem.at[6 + d], b + (zp - z) * NY, r))

    def from_above():
        low_out.wait_recv()
        term_own[...] += relay_r[0].astype(F32)

    def from_below():
        high_out.wait_recv()
        term_own[...] += relay_r[1].astype(F32)

    pl.when(y >= 1)(from_above)
    pl.when(y <= 1)(from_below)
    onto = hot(iota((D, 256), 0) == rows[10:11, :])
    high, low = two_parts(term_own[...])
    part = mm(onto, high) + mm(onto, low)
    for c in range(4):
        loc[c] += part[:, c * 128 : (c + 1) * 128]
        loc_s[c] = loc[c].astype(BF16)
    rep_out = []
    for d in range(1, NREP):
        rp = lax.rem(r + d, NREP)
        rep_out.append(send(loc_s.at[rp], loc_r.at[d - 1], rep_sem.at[d - 1], rep_sem.at[2 + d], b, rp))

    total = rz_f[:, pl.ds(pl.multiple_of(z * 16, 16), 16), :]
    for d in range(1, NZ):
        z_out[d - 1].wait_recv()
        total += rz_r[d - 1].astype(F32)
    for x in range(NX):
        rx_s[x] = total[:, x * 8 : (x + 1) * 8, :]
    x_out = send(rx_s.at[xp], rx_r, x_sem.at[4], x_sem.at[5], other_x, r)
    total = loc[r]
    for d in range(1, NREP):
        rep_out[d - 1].wait_recv()
        total += loc_r[d - 1].astype(F32)
    out_e[...] = total

    for k in range(2):
        out_r[2 * xl + k] = rx_s[xl, k]
    x_out.wait_recv()
    for k in range(2):
        out_r[2 * xp + k] = rx_r[k]

    pl.when(y >= 1)(up_out.wait_send)
    pl.when(y <= 1)(down_out.wait_send)
    pl.when(y >= 1)(low_out.wait_send)
    pl.when(y <= 1)(high_out.wait_send)
    pl.when(y == 2)(block_out[2].wait_send)
    pl.when(y == 1)(block_out[3].wait_send)
    pl.when(y <= 2)(on_up.wait_send)
    pl.when(y >= 1)(on_down.wait_send)
    for copy in (block_out[0], block_out[1], block_out[4], head_out, *term_out, pair_out, *y_out, *rep_out, *z_out, x_out):
        copy.wait_send()
    wait_all(asked.at[pl.ds(0, NBLK - 1)], a2a_sem.at[0])
    wait_all(served.at[pl.ds(0, (NBLK - 1) * 16)], a2a_sem.at[2])
    wait_all(back_s.at[pl.ds(0, (NBLK - 1) * 16)], a2a_sem.at[4])


def per_device(entity, relation, head_owner, head_row, query_rel, tail_row, neg_row):
    vmem = pl.BlockSpec(memory_space=pltpu.VMEM)
    dma = pltpu.SemaphoreType.DMA
    scratch = [
        pltpu.VMEM((D, D), BF16),
        pltpu.VMEM((4, D, D), BF16),
        pltpu.VMEM((1, 256), I32),
        pltpu.VMEM((1, 256), I32),
        pltpu.VMEM((4, 256), I32),
        pltpu.VMEM((4, 256), I32),
        pltpu.VMEM((1, 256), I32),
        pltpu.VMEM((128, 256), I32),
        pltpu.VMEM((256, 128), I32),
        pltpu.VMEM((NBLK, 1, 128), F32),
        pltpu.VMEM((NBLK, 1, 128), F32),
        pltpu.VMEM((NBLK, 128), F32),
        pltpu.VMEM((8, 1024), I32),
        pltpu.VMEM((1024, 256), BF16),
        pltpu.VMEM((1024, 256), BF16),
        pltpu.VMEM((STOPS * 256, D), BF16),
        pltpu.VMEM((2, 256, D), BF16),
        pltpu.VMEM((1024, D), BF16),
        pltpu.VMEM((256, D), BF16),
        pltpu.VMEM((D, 256), BF16),
        pltpu.VMEM((D, 256), BF16),
        pltpu.VMEM((4, 256, D), F32),
        pltpu.VMEM((1024, D), BF16),
        pltpu.VMEM((1024, 128), F32),
        pltpu.VMEM((1024, D), F32),
        pltpu.VMEM((1024, STOPS * 256), BF16),
        pltpu.VMEM((4, 256, D), BF16),
        pltpu.VMEM((2, 256, D), BF16),
        pltpu.VMEM((256, D), F32),
        pltpu.VMEM((STOPS - 1, 256, D), BF16),
        pltpu.VMEM((STOPS - 1, 256, D), BF16),
        pltpu.VMEM((2, 256, D), F32),
        pltpu.VMEM((2, 256, D), BF16),
        pltpu.VMEM((2, 256, D), BF16),
        pltpu.VMEM((1024, 256), BF16),
        pltpu.VMEM((1024, 256), BF16),
        pltpu.VMEM((2, D, D), F32),
        pltpu.VMEM((2, D, D), BF16),
        pltpu.VMEM((NY - 1, 2, 128, D), BF16),
        pltpu.VMEM((2, 128, D), F32),
        pltpu.VMEM((2, 128, D), BF16),
        pltpu.VMEM((NZ - 1, 2, 16, D), BF16),
        pltpu.VMEM((NX, 2, 8, D), F32),
        pltpu.VMEM((2, 8, D), F32),
        pltpu.VMEM((4, D, 128), F32),
        pltpu.VMEM((4, D, 128), BF16),
        pltpu.VMEM((NREP - 1, D, 128), BF16),
        dma((7,)),
        dma((6,)),
        dma((10,)),
        dma((2,)),
        dma((10,)),
        dma((8,)),
        dma((6,)),
        dma((6,)),
        dma((14,)),
        dma((6,)),
    ]
    return pl.pallas_call(
        kernel,
        out_shape=(jax.ShapeDtypeStruct((D, 128), F32), jax.ShapeDtypeStruct((4, 8, D), F32)),
        in_specs=[pl.BlockSpec(memory_space=pl.ANY)] * 7,
        out_specs=(vmem, vmem),
        scratch_shapes=scratch,
        compiler_params=pltpu.CompilerParams(
            collective_id=0, has_side_effects=True, vmem_limit_bytes=61 * 2**20
        ),
        name="rescal_step",
    )(entity, relation, head_owner.T, head_row[None, :], query_rel.T, tail_row.T, neg_row)


def solution(mesh):
    placed = (
        P("blk", None),
        P("rep", None, None),
        P(("blk", "rep"), None),
        P(("blk", "rep")),
        P(("blk", "rep"), None),
        P(("blk", "rep"), None),
        P("blk", "rep"),
    )
    return jax.shard_map(
        per_device,
        mesh=mesh,
        in_specs=placed,
        out_specs=(P("blk", "rep"), P("rep", "blk", None)),
        check_vma=False,
    )
```
